32 devices in a mesh: section: 2 (over core), dp: 16 (over z, y, x).
Axes of the slice: x: 2, y: 2, z: 4, core: 2. Of those that a mesh axis runs over, the one named last changes fastest.
Arguments:
- boards: bfloat16 [6, 48, 19, 19, 256], P(None, 'dp'), may hold values from -17 to 17
- cotangent: bfloat16 [6, 48, 19, 19, 256], P(None, 'dp'), may hold values from -6 to 6
- counts: int32 [6, 16], P(None, 'dp'), may hold values from 1 to 3, as said below
- kernel_one: bfloat16 [2, 3, 3, 256, 256], P('section'), may hold values from -0.125 to 0.125
- kernel_two: bfloat16 [2, 3, 3, 256, 256], P('section'), may hold values from -0.125 to 0.125
- gains: float32 [2, 2, 256], P('section'), may hold values from 0.25 to 1.75
- biases: float32 [2, 2, 256], P('section'), may hold values from -3 to 3
Outputs:
- hidden: bfloat16 [2, 6, 48, 19, 19, 256], P('section', None, 'dp')
- input_grads: bfloat16 [2, 6, 48, 19, 19, 256], P('section', None, 'dp')
- kernel_one_grad: float32 [2, 3, 3, 256, 256], P('section')
- kernel_two_grad: float32 [2, 3, 3, 256, 256], P('section')
- gain_grad: float32 [2, 2, 256], P('section')
- bias_grad: float32 [2, 2, 256], P('section')
The draws below stay inside these ranges and needn't reach their ends.
Inputs may be any that keep to these rules, and one draw needn't show every extreme that they name: `counts`: in every micro-batch some device has all 3 slots filled.
All inputs are finite; a program needn't handle non-finite values.
Results may differ from the reference program's by a relative error of at most 0.008.
Values may be sent and summed in bfloat16 or wider, within the bound.
A program may use at most 256 MiB of HBM per device.

```python
import jax
import jax.numpy as jnp
from jax import lax

C = 256
BOARD = 19
SLOTS = 3
MICRO = 6
POSITIONS = 48


def draw_boards(key, part):
    key = jax.random.fold_in(key, 11)
    noise_key, offset_key = jax.random.split(key)
    shape = (MICRO, POSITIONS, BOARD, BOARD, C)
    device_rank = (jnp.arange(POSITIONS) // SLOTS).astype(jnp.float32)
    devices = POSITIONS // SLOTS
    growth = 3.0 ** (device_rank / max(devices - 1, 1))
    offsets = jnp.clip(0.5 * jax.random.normal(offset_key, (C,), jnp.float32), -1.5, 1.5)
    noise = jnp.clip(jax.random.normal(noise_key, shape, jnp.float32), -4.0, 4.0)
    return (growth[None, :, None, None, None] * (noise + offsets)).astype(jnp.bfloat16)


def draw_counts(key, part):
    key = jax.random.fold_in(key, 23)
    first_key, second_key = jax.random.split(key)
    devices = POSITIONS // SLOTS
    drawn = jax.random.randint(first_key, (MICRO, devices), 1, SLOTS + 1)
    fullest = jax.random.randint(second_key, (MICRO, 1), 0, devices)
    return jnp.where(jnp.arange(devices)[None, :] == fullest, SLOTS, drawn).astype(jnp.int32)


def levels(key, dims, cuts, smallest, top_value):
    loudness, own = 1.0, jax.random.fold_in(key, 6)
    for position, shards_of in cuts:
        draws = jnp.exp(jax.random.uniform(jax.random.fold_in(own, position), (shards_of,), jnp.float32, smallest / len(cuts), top_value / len(cuts)))
        loudness = loudness * jnp.repeat(draws, dims[position] // shards_of).reshape([-1 if axis == position else 1 for axis in range(len(dims))])
    return loudness


def normal_values(own_key, extent, deviation, reach, cuts=(), kind=jnp.bfloat16):
    entries = deviation * jax.random.normal(own_key, extent, jnp.float32)
    if cuts:
        entries = entries * levels(own_key, extent, cuts, -0.22, 0.18)
    return jnp.clip(entries, -reach, reach).astype(kind)


def setup_inputs(seed: int = 0) -> dict:
    keys = jax.random.split(jax.random.key(seed), 8)
    boards = draw_boards(jax.random.fold_in(keys[7], 71), 0)
    cotangent = normal_values(keys[1], (MICRO, POSITIONS, BOARD, BOARD, C), 1.0, 6.0, ((1, 16),))
    counts = draw_counts(jax.random.fold_in(keys[7], 71), 0)
    kernel_one = normal_values(keys[3], (2, 3, 3, C, C), (9 * C) ** -0.5, 0.125, ((0, 2),))
    kernel_two = normal_values(keys[4], (2, 3, 3, C, C), (9 * C) ** -0.5, 0.125, ((0, 2),))
    gains = jnp.clip(1.0 + 0.15 * jax.random.normal(keys[5], (2, 2, C), jnp.float32), 0.25, 1.75)
    biases = normal_values(keys[6], (2, 2, C), 0.5, 3.0, ((0, 2),), jnp.float32)
    return {"boards": boards, "cotangent": cotangent, "counts": counts, "kernel_one": kernel_one, "kernel_two": kernel_two, "gains": gains, "biases": biases}


@jax.custom_vjp
def low(v):
    return lax.optimization_barrier(v.astype(jnp.bfloat16)).astype(jnp.float32)

@jax.custom_vjp
def low_back(v):
    return v

def low_keep(v):
    return (low(v), None)

def low_pass(kept, grad):
    return (grad,)

def back_keep(v):
    return (v, None)

def back_low(kept, grad):
    return (low(grad),)
low.defvjp(low_keep, low_pass)
low_back.defvjp(back_keep, back_low)

def convolution(values, kernel):
    return lax.conv_general_dilated(values, kernel, (1, 1), 'SAME', dimension_numbers=('NHWC', 'HWIO', 'NHWC'), precision=lax.Precision.HIGHEST)

def batch_norm(field, slot_mask, count_all, gain_row, bias_row):
    first_sum = lax.optimization_barrier(jnp.sum(slot_mask * field, axis=(0, 1, 2)))
    second_sum = lax.optimization_barrier(jnp.sum(slot_mask * field * field, axis=(0, 1, 2)))
    average = first_sum / count_all
    variance = second_sum / count_all - average * average
    scale_inv = lax.rsqrt(variance + 1e-05)
    return (field - average) * scale_inv * gain_row + bias_row

def residual_block(values, first_kernel, second_kernel, gain_pair, bias_pair, slot_mask, count_all):
    values = low_back(values)
    first_conv = low_back(convolution(values, first_kernel))
    first_norm = batch_norm(first_conv, slot_mask, count_all, gain_pair[0], bias_pair[0])
    activated = low(jax.nn.silu(first_norm))
    second_conv = low_back(convolution(activated, second_kernel))
    second_norm = batch_norm(second_conv, slot_mask, count_all, gain_pair[1], bias_pair[1])
    return low(jax.nn.silu(second_norm + values) * slot_mask)

def reference(boards, cotangent, counts, kernel_one, kernel_two, gains, biases):
    boards_wide = boards.astype(jnp.float32)
    cot_wide = cotangent.astype(jnp.float32)
    kernel_first = kernel_one.astype(jnp.float32)
    kernel_second = kernel_two.astype(jnp.float32)
    slot_masks = []
    count_alls = []
    for batch in range(MICRO):
        filled = (jnp.arange(SLOTS, dtype=jnp.int32)[None, :] < counts[batch][:, None]).astype(jnp.float32)
        slot_masks.append(filled.reshape(POSITIONS, 1, 1, 1))
        count_alls.append(jnp.sum(counts[batch]).astype(jnp.float32) * (BOARD * BOARD))

    def forward(inputs, offsets, first_kernels, second_kernels, gain_all, bias_all):
        firsts = []
        seconds = []
        for batch in range(MICRO):
            middle = residual_block(inputs[batch], first_kernels[0], second_kernels[0], gain_all[0], bias_all[0], slot_masks[batch], count_alls[batch])
            ending = residual_block(middle + offsets[batch], first_kernels[1], second_kernels[1], gain_all[1], bias_all[1], slot_masks[batch], count_alls[batch])
            firsts.append(middle)
            seconds.append(ending)
        return (jnp.stack(firsts), jnp.stack(seconds))
    outputs, pullback = jax.vjp(forward, boards_wide, jnp.zeros_like(boards_wide), kernel_first, kernel_second, gains, biases)
    grads = pullback((jnp.zeros_like(outputs[0]), cot_wide))
    hidden = jnp.stack([outputs[0], outputs[1]]).astype(jnp.bfloat16)
    input_grads = jnp.stack([grads[0], grads[1]]).astype(jnp.bfloat16)
    return (hidden, input_grads, grads[2], grads[3], grads[4], grads[5])
```

```python
import functools

import jax
import jax.numpy as jnp
from jax import lax
from jax.experimental import pallas as pl
from jax.experimental.pallas import tpu as pltpu
from jax.sharding import PartitionSpec as P

MESH = pl.DeviceIdType.MESH
F32, BF16 = jnp.float32, jnp.bfloat16

STRIPS, AI, TILE = 5, 4, 16


class Plan:
    pass


def kernel(g, *refs):
    (
        boards, cot, counts, kone, ktwo, gains, biases,
        hidden, igrads, kout1, kout2, gout, bout,
        stage, ostage, temp, xs, us, ds, h1, h2, dp_, dy_, w1, w2, gb, coef, masks, acc, msg, inbox, psend, precv, gacc, grecv,
        sem_in, sem_cot, sem_w, sem_wr, sem_ws, sem_out, sem_outr, sem_msg, sem_inbox, sem_ps, sem_pr,
    ) = refs
    n, micro, slots, board, C = g.n, g.half, g.slots, g.board, g.channels
    BT = board * TILE
    me = lax.axis_index("dp")
    sec = lax.axis_index("section")
    other = 1 - sec
    partner = {"section": other}
    first = sec * micro

    for m in range(micro):
        pltpu.make_async_copy(boards.at[first + m], stage.at[m], sem_in.at[m]).start()
    own_w = [
        pltpu.make_async_copy(kone.at[0], w1.at[sec], sem_w.at[0]),
        pltpu.make_async_copy(ktwo.at[0], w2.at[sec], sem_w.at[1]),
        pltpu.make_async_copy(gains.at[0], gb.at[sec, 0], sem_w.at[2]),
        pltpu.make_async_copy(biases.at[0], gb.at[sec, 1], sem_w.at[3]),
    ]
    for c in own_w:
        c.start()
    barrier = pltpu.get_barrier_semaphore()

    def greet(i, _):
        pl.semaphore_signal(barrier, inc=1, device_id={"dp": lax.rem(me + i, n)}, device_id_type=MESH)
        return 0

    lax.fori_loop(1, n, greet, 0)
    pl.semaphore_signal(barrier, inc=1, device_id=partner, device_id_type=MESH)
    pl.semaphore_wait(barrier, n)
    send_w = [
        pltpu.make_async_remote_copy(kone.at[0], w1.at[sec], sem_ws.at[0], sem_wr.at[0], device_id=partner, device_id_type=MESH),
        pltpu.make_async_remote_copy(gains.at[0], gb.at[sec, 0], sem_ws.at[2], sem_wr.at[2], device_id=partner, device_id_type=MESH),
        pltpu.make_async_remote_copy(biases.at[0], gb.at[sec, 1], sem_ws.at[3], sem_wr.at[3], device_id=partner, device_id_type=MESH),
        pltpu.make_async_remote_copy(ktwo.at[0], w2.at[sec], sem_ws.at[1], sem_wr.at[1], device_id=partner, device_id_type=MESH),
    ]
    for c in send_w:
        c.start()

    entry = lax.broadcasted_iota(jnp.int32, (TILE, C), 0)
    slot = lax.rem(entry, slots)
    for m in range(micro):
        filled = jnp.logical_and(slot < counts[first + m, 0], entry < STRIPS * slots)
        masks[m, 0] = filled.astype(F32)
        masks[m, 1] = jnp.logical_and(filled, entry < (STRIPS - 1) * slots).astype(F32)

    edge = jnp.zeros((6, TILE, C), BF16)

    def clear(m, _):
        for ref in (xs.at[0], xs.at[1], us.at[0], us.at[1]):
            ref[m, :, pl.ds(0, TILE), :] = edge
            ref[m, :, pl.ds((board + 1) * TILE, TILE), :] = edge
        return 0

    lax.fori_loop(0, micro, clear, 0)
    ds[:, pl.ds(0, TILE), :] = edge
    ds[:, pl.ds((board + 1) * TILE, TILE), :] = edge

    def clear_acc(t, _):
        for k in range(2):
            for j in range(2):
                acc[k, j, t] = jnp.zeros((C, C), F32)
        return 0

    lax.fori_loop(0, 9, clear_acc, 0)
    temp[...] = jnp.zeros_like(temp)
    gacc[...] = jnp.zeros_like(gacc)

    def mask_of(m, ai):
        return masks[m, 1 if ai == AI - 1 else 0][None]

    def tiles(v):
        return v.reshape(board, TILE, C)

    def flat(v):
        return v.reshape(BT, C)

    def put(ref, ai, value):
        ref[ai + 1, pl.ds(TILE, BT), :] = flat(value).astype(BF16)
        if ai == AI - 1:
            ref[0, pl.ds(TILE, BT), :] = flat(pltpu.roll(value, slots, 1)).astype(BF16)
        if ai == 0:
            ref[AI + 1, pl.ds(TILE, BT), :] = flat(pltpu.roll(value, TILE - slots, 1)).astype(BF16)

    def window(ref, ai, i, j):
        return ref[ai + i, pl.ds(j * TILE, BT), :]

    def inner(ref, ai):
        return window(ref, ai, 1, 1)

    def conv(ref, ai, weights):
        lhs = jnp.concatenate([window(ref, ai, i, j) for i in range(3) for j in range(3)], axis=1)
        return jnp.dot(lhs, weights[...].reshape(9 * C, C), preferred_element_type=F32)

    def conv_back(ref, ai, weights):
        out = None
        for i in range(3):
            for j in range(3):
                part = lax.dot_general(
                    window(ref, ai, i, j), weights[(2 - i) * 3 + 2 - j], (((1,), (1,)), ((), ())), preferred_element_type=F32
                )
                out = part if out is None else out + part
        return out

    def kernel_grad(total, ref, grad):
        lhs = jnp.concatenate([inner(ref, ai) for ai in range(AI)], axis=0)
        for i in range(3):
            for j in range(3):
                rhs = jnp.concatenate([window(grad, ai, 2 - i, 2 - j) for ai in range(AI)], axis=0)
                total[i * 3 + j] += lax.dot_general(lhs, rhs, (((0,), (0,)), ((), ())), preferred_element_type=F32)

    def fold(v):
        return jnp.sum(v.reshape(BT // 8, 8, C), axis=0)

    def send_stats(phase, m, one, two):
        par = phase % 2
        one = jnp.sum(one, axis=0, keepdims=True)
        two = jnp.sum(two, axis=0, keepdims=True)
        here = counts[first + m, 0].astype(F32) * float(board * board)
        rows = [one[:, :128], one[:, 128:], two[:, :128], two[:, 128:]]
        for r, v in enumerate(rows):
            msg[par, m, pl.ds(r, 1), :] = v
        msg[par, m, pl.ds(4, 4), :] = jnp.full((4, 128), here, F32)
        inbox[par, m, me] = msg[par, m]

        def ship(i, _):
            pltpu.make_async_remote_copy(
                msg.at[par, m], inbox.at[par, m, me], sem_msg.at[par, m], sem_inbox.at[par, m],
                device_id={"dp": lax.rem(me + i, n)}, device_id_type=MESH,
            ).start()
            return 0

        lax.fori_loop(1, n, ship, 0, unroll=n <= 16)

    def get_stats(phase, m):
        par = phase % 2
        several = inbox.at[par, m, pl.ds(0, n - 1)]
        pltpu.make_async_copy(several, several, sem_inbox.at[par, m]).wait()
        pltpu.make_async_copy(several, several, sem_msg.at[par, m]).wait()
        if n <= 16:
            total = inbox[par, m, 0]
            for d in range(1, n):
                total = total + inbox[par, m, d]
        else:
            total = jnp.sum(inbox[par, m], axis=0)
        one = jnp.concatenate([total[0:1], total[1:2]], axis=1)
        two = jnp.concatenate([total[2:3], total[3:4]], axis=1)
        count = jnp.concatenate([total[4:5], total[4:5]], axis=1)
        return one, two, count

    def norm_coefs(phase, m, k, j):
        one, two, count = get_stats(phase, m)
        mean = one / count
        var = two / count - mean * mean
        r = lax.rsqrt(var + 1e-5)
        scale = r * gb[k, 0, pl.ds(j, 1), :]
        offset = gb[k, 1, pl.ds(j, 1), :] - mean * scale
        for q, v in enumerate((0.5 * scale, 0.5 * offset, r, mean, count, scale)):
            coef[k, j, m, pl.ds(q, 1), :] = v
        return 0.5 * scale, 0.5 * offset

    def kept(m, k, j):
        return coef[k, j, m, pl.ds(0, 1), :], coef[k, j, m, pl.ds(1, 1), :]

    def back_coefs(phase, m, k, j):
        sdy, sdh, _ = get_stats(phase, m)
        r, mean = coef[k, j, m, pl.ds(2, 1), :], coef[k, j, m, pl.ds(3, 1), :]
        count, alpha = coef[k, j, m, pl.ds(4, 1), :], coef[k, j, m, pl.ds(5, 1), :]
        sdx = r * (sdh - mean * sdy)
        gacc[k, 0, pl.ds(j, 1), :] += sdx
        gacc[k, 1, pl.ds(j, 1), :] += sdy
        gamma = -alpha * r * sdx / count
        beta = -alpha * sdy / count - gamma * mean
        return alpha, gamma, beta

    def silu2(z):
        return z + z * jnp.tanh(z)

    def slope2(z):
        t = jnp.tanh(z)
        return (0.5 + 0.5 * t) * (1.0 + z * (1.0 - t))

    def places():
        return [(p, a) for p in range(slots) for a in range(board)]

    def spread(m):
        for p, a in places():
            rows = pl.ds(a // AI * slots + p, board, TILE)
            for c in range(C // 128):
                temp[c, a % AI, rows, :] = stage[m, p, a, :, pl.ds(128 * c, 128)].astype(F32)

    def gather(m):
        for p, a in places():
            rows = pl.ds(a // AI * slots + p, board, TILE)
            for c in range(C // 128):
                ostage[m, p, a, :, pl.ds(128 * c, 128)] = temp[c, a % AI, rows, :].astype(BF16)

    def read_temp(ai):
        return jnp.concatenate([temp[c, ai] for c in range(C // 128)], axis=1)

    def write_temp(ai, v):
        for c in range(C // 128):
            temp[c, ai] = v[:, 128 * c : 128 * (c + 1)]

    def wait_out(m):
        pltpu.make_async_copy(ostage.at[m], ostage.at[m], sem_out.at[m]).wait()

    def emit(which, k, m):
        out = (hidden, igrads)[which]

        @pl.when(sec == k)
        def _():
            pltpu.make_async_copy(ostage.at[m], out.at[0, first + m], sem_out.at[m]).start()

        @pl.when(sec != k)
        def _():
            pltpu.make_async_remote_copy(
                ostage.at[m], out.at[0, first + m], sem_out.at[m], sem_outr.at[which, m], device_id=partner, device_id_type=MESH
            ).start()

    def each(body):
        def step(m, _):
            body(m)
            return 0

        lax.fori_loop(0, micro, step, 0)

    def run_conv(phase, m, ref, weights, target):
        one = two = jnp.zeros((8, C), F32)
        for ai in range(AI):
            h = conv(ref, ai, weights)
            target[ai] = h
            if ai == AI - 1:
                h = flat(tiles(h) * mask_of(m, ai))
            one = one + fold(h)
            two = two + fold(h * h)
        send_stats(phase, m, one, two)

    ORDER = (AI - 1,) + tuple(range(AI - 1))

    def first_conv(m):
        pltpu.make_async_copy(stage.at[m], stage.at[m], sem_in.at[m]).wait()
        spread(m)
        pltpu.make_async_copy(cot.at[first + m], stage.at[m], sem_cot.at[m]).start()
        for ai in ORDER:
            put(xs.at[0, m], ai, tiles(read_temp(ai)) * mask_of(m, ai))
        run_conv(0, m, xs.at[0, m], w1.at[0], h1.at[0, m])

    def second_conv(phase, k):
        def body(m):
            a, b = norm_coefs(phase - 1, m, k, 0)
            for ai in ORDER:
                put(us.at[k, m], ai, tiles(silu2(h1[k, m, ai] * a + b)) * mask_of(m, ai))
            run_conv(phase, m, us.at[k, m], w2.at[k], h2.at[k, m])

        return body

    def third_conv(m):
        a, b = norm_coefs(1, m, 0, 1)
        for ai in ORDER:
            z = h2[0, m, ai] * a + b + 0.5 * inner(xs.at[0, m], ai).astype(F32)
            x = tiles(silu2(z)) * mask_of(m, ai)
            put(xs.at[1, m], ai, x)
            write_temp(ai, flat(x))
        run_conv(2, m, xs.at[1, m], w1.at[1], h1.at[1, m])
        gather(m)
        emit(0, 0, m)

    def turn(m):
        a, b = norm_coefs(3, m, 1, 1)
        wait_out(m)
        for ai in range(AI):
            z = h2[1, m, ai] * a + b + 0.5 * inner(xs.at[1, m], ai).astype(F32)
            write_temp(ai, flat(tiles(silu2(z)) * mask_of(m, ai)))
        gather(m)
        emit(0, 1, m)
        pltpu.make_async_copy(stage.at[m], stage.at[m], sem_cot.at[m]).wait()
        write_temp(AI - 1, jnp.zeros((BT, C), F32))
        spread(m)
        one = two = jnp.zeros((8, C), F32)
        for ai in range(AI):
            h = h2[1, m, ai]
            z = h * a + b + 0.5 * inner(xs.at[1, m], ai).astype(F32)
            dy = flat(tiles(read_temp(ai) * slope2(z)) * mask_of(m, ai))
            dp_[m, ai] = dy
            one = one + fold(dy)
            two = two + fold(dy * h)
        send_stats(4, m, one, two)

    def back_second(phase, k):
        def body(m):
            alpha, gamma, beta = back_coefs(phase - 1, m, k, 1)
            for ai in ORDER:
                put(ds, ai, tiles(alpha * dp_[m, ai] + gamma * h2[k, m, ai] + beta) * mask_of(m, ai))
            a, b = kept(m, k, 0)
            one = two = jnp.zeros((8, C), F32)
            for ai in range(AI):
                du = conv_back(ds, ai, w2.at[k])
                h = h1[k, m, ai]
                dy = du * slope2(h * a + b)
                if ai == AI - 1:
                    dy = flat(tiles(dy) * mask_of(m, ai))
                dy_[m, ai] = dy
                one = one + fold(dy)
                two = two + fold(dy * h)
            send_stats(phase, m, one, two)
            kernel_grad(acc.at[k, 1], us.at[k, m], ds)

        return body

    def back_first(phase, k):
        def body(m):
            alpha, gamma, beta = back_coefs(phase - 1, m, k, 0)
            wait_out(m)
            for ai in ORDER:
                put(ds, ai, tiles(alpha * dy_[m, ai] + gamma * h1[k, m, ai] + beta) * mask_of(m, ai))
            if k == 1:
                a, b = kept(m, 0, 1)
                one = two = jnp.zeros((8, C), F32)
            for ai in range(AI):
                dx = (conv_back(ds, ai, w1.at[k]) + dp_[m, ai]).astype(BF16).astype(F32)
                write_temp(ai, dx)
                if k == 1:
                    h = h2[0, m, ai]
                    z = h * a + b + 0.5 * inner(xs.at[0, m], ai).astype(F32)
                    dy = dx * slope2(z)
                    if ai == AI - 1:
                        dy = flat(tiles(dy) * mask_of(m, ai))
                    dp_[m, ai] = dy
                    one = one + fold(dy)
                    two = two + fold(dy * h)
            if k == 1:
                send_stats(phase, m, one, two)
            gather(m)
            emit(1, k, m)
            kernel_grad(acc.at[k, 0], xs.at[k, m], ds)

        return body

    def pair(k, j, kout):
        @pl.when(sec != k)
        def _():
            def cast(t, _):
                psend[j, t] = acc[k, j, t].astype(BF16)
                return 0

            lax.fori_loop(0, 9, cast, 0)
            pltpu.make_async_remote_copy(
                psend.at[j], precv.at[j], sem_ps.at[j], sem_pr.at[j], device_id=partner, device_id_type=MESH
            ).start()

    @pl.when(sec == 0)
    def _():
        pltpu.make_async_copy(kone.at[0], w1.at[sec], sem_w.at[0]).wait()

    @pl.when(sec != 0)
    def _():
        pltpu.make_async_copy(w1.at[other], w1.at[other], sem_wr.at[0]).wait()

    each(first_conv)
    for c in own_w[1:]:
        c.wait()

    @pl.when(sec != 0)
    def _():
        own_w[0].wait()

    for ref, q in ((w2.at[other], 1), (gb.at[other, 0], 2), (gb.at[other, 1], 3)):
        pltpu.make_async_copy(ref, ref, sem_wr.at[q]).wait()

    each(second_conv(1, 0))

    @pl.when(sec == 0)
    def _():
        pltpu.make_async_copy(w1.at[other], w1.at[other], sem_wr.at[0]).wait()

    for c in send_w:
        c.wait_send()
    each(third_conv)
    each(second_conv(3, 1))
    each(turn)
    each(back_second(5, 1))
    pair(1, 1, kout2)
    each(back_first(6, 1))
    pair(1, 0, kout1)
    each(back_second(7, 0))
    pair(0, 1, kout2)
    each(back_first(8, 0))
    pair(0, 0, kout1)

    give = pltpu.make_async_remote_copy(gacc.at[other], grecv, sem_ps.at[2], sem_pr.at[2], device_id=partner, device_id_type=MESH)
    give.start()
    outs = []
    for j, kout in ((1, kout2), (0, kout1)):
        pltpu.make_async_copy(precv.at[j], precv.at[j], sem_pr.at[j]).wait()

        def add(t, _):
            acc[sec, j, t] += precv[j, t].astype(F32)
            return 0

        lax.fori_loop(0, 9, add, 0)
        c = pltpu.make_async_copy(acc.at[sec, j], kout.at[0], sem_w.at[j])
        c.start()
        outs.append(c)
    give.wait()
    gout[0] = gacc[sec, 0] + grecv[0]
    bout[0] = gacc[sec, 1] + grecv[1]
    for m in range(micro):
        wait_out(m)
    for which, out in enumerate((hidden, igrads)):
        for m in range(micro):
            came = out.at[0, other * micro + m]
            pltpu.make_async_copy(came, came, sem_outr.at[which, m]).wait()
    for j in range(2):
        pltpu.make_async_copy(psend.at[j], psend.at[j], sem_ps.at[j]).wait()
    for c in outs:
        c.wait()


def local(n, boards, cotangent, counts, kernel_one, kernel_two, gains, biases):
    g = Plan()
    micro, slots, board, _, C = boards.shape
    g.n, g.half, g.slots, g.board, g.channels = n, micro // 2, slots, board, C
    half = g.half
    BT = board * TILE
    haloed = (AI + 2, (board + 2) * TILE, C)
    dense = (AI, BT, C)
    flat_kernel = (1, 9, C, C)
    dma = pltpu.SemaphoreType.DMA
    scratch = [
        pltpu.VMEM((half, slots, board, board, C), BF16),
        pltpu.VMEM((half, slots, board, board, C), BF16),
        pltpu.VMEM((C // 128, AI, BT, 128), F32),
        pltpu.VMEM((2, half) + haloed, BF16),
        pltpu.VMEM((2, half) + haloed, BF16),
        pltpu.VMEM(haloed, BF16),
        pltpu.VMEM((2, half) + dense, F32),
        pltpu.VMEM((2, half) + dense, F32),
        pltpu.VMEM((half,) + dense, F32),
        pltpu.VMEM((half,) + dense, F32),
        pltpu.VMEM((2, 9, C, C), BF16),
        pltpu.VMEM((2, 9, C, C), BF16),
        pltpu.VMEM((2, 2, 2, C), F32),
        pltpu.VMEM((2, 2, half, 8, C), F32),
        pltpu.VMEM((half, 2, TILE, C), F32),
        pltpu.VMEM((2, 2, 9, C, C), F32),
        pltpu.VMEM((2, half, 8, 128), F32),
        pltpu.VMEM((2, half, n, 8, 128), F32),
        pltpu.VMEM((2, 9, C, C), BF16),
        pltpu.VMEM((2, 9, C, C), BF16),
        pltpu.VMEM((2, 2, 2, C), F32),
        pltpu.VMEM((2, 2, C), F32),
        dma((half,)), dma((half,)), dma((4,)), dma((4,)), dma((4,)),
        dma((half,)), dma((2, half)), dma((2, half)), dma((2, half)), dma((3,)), dma((3,)),
    ]
    anywhere = pl.BlockSpec(memory_space=pl.ANY)
    vmem = pl.BlockSpec(memory_space=pltpu.VMEM)
    smem = pl.BlockSpec(memory_space=pltpu.SMEM)
    field = jax.ShapeDtypeStruct((1,) + boards.shape, BF16)
    grad = jax.ShapeDtypeStruct(flat_kernel, F32)
    pair = jax.ShapeDtypeStruct(gains.shape, F32)
    hidden, igrads, k1, k2, gg, bg = pl.pallas_call(
        functools.partial(kernel, g),
        out_shape=(field, field, grad, grad, pair, pair),
        in_specs=[anywhere, anywhere, smem, anywhere, anywhere, anywhere, anywhere],
        out_specs=(anywhere, anywhere, anywhere, anywhere, vmem, vmem),
        scratch_shapes=scratch,
        compiler_params=pltpu.CompilerParams(collective_id=0, has_side_effects=True, vmem_limit_bytes=63 * 2**20),
    )(
        boards, cotangent, counts, kernel_one.reshape(flat_kernel), kernel_two.reshape(flat_kernel), gains, biases
    )
    k1, k2 = lax.psum((k1, k2), "dp")
    return hidden, igrads, k1.reshape(kernel_one.shape), k2.reshape(kernel_two.shape), gg, bg


def solution(mesh):
    return jax.shard_map(
        functools.partial(local, mesh.shape["dp"]),
        mesh=mesh,
        in_specs=(
            P(None, "dp", None, None, None),
            P(None, "dp", None, None, None),
            P(None, "dp"),
            P("section", None, None, None, None),
            P("section", None, None, None, None),
            P("section", None, None),
            P("section", None, None),
        ),
        out_specs=(
            P("section", None, "dp", None, None, None),
            P("section", None, "dp", None, None, None),
            P("section", None, None, None, None),
            P("section", None, None, None, None),
            P("section", None, None),
            P("section", None, None),
        ),
        check_vma=False,
    )
```

```python
import functools

import jax
import jax.numpy as jnp
from jax import lax
from jax.experimental import pallas as pl
from jax.experimental.pallas import tpu as pltpu
from jax.sharding import PartitionSpec as P

MESH = pl.DeviceIdType.MESH
F32, BF16 = jnp.float32, jnp.bfloat16

STRIPS, AI, TILE = 5, 4, 16


class Plan:
    pass


def kernel(g, *refs):
    (
        boards, cot, counts, kone, ktwo, gains, biases,
        hidden, igrads, kout1, kout2, gout, bout,
        stage, ostage, temp, xs, us, ds, h1, h2, dp_, w1, w2, gb, coef, masks, acc, msg, inbox, cmsg, cinbox, totals, gacc, grecv, filled_here,
        psend, precv, xsend, xrecv, ysend, yrecv, zsend, zrecv, rrecv, result,
        sem_in, sem_cot, sem_w, sem_wr, sem_ws, sem_out, sem_outr, sem_msg, sem_inbox, sem_c, sem_g, sem_js, sem_jr, sem_res, sem_free,
    ) = refs
    dy_ = h2.at[1]
    n, micro, slots, board, C = g.n, g.half, g.slots, g.board, g.channels
    BT = board * TILE
    me = lax.axis_index("dp")
    sec = lax.axis_index("section")
    other = 1 - sec
    partner = {"section": other}
    first = sec * micro

    for m in range(micro):
        pltpu.make_async_copy(boards.at[first + m], stage.at[m], sem_in.at[m]).start()
    count_in = pltpu.make_async_copy(counts, filled_here, sem_w.at[4])
    count_in.start()
    own_w = [
        pltpu.make_async_copy(kone.at[0], w1.at[sec], sem_w.at[0]),
        pltpu.make_async_copy(ktwo.at[0], w2.at[sec], sem_w.at[1]),
        pltpu.make_async_copy(gains.at[0], gb.at[sec, 0], sem_w.at[2]),
        pltpu.make_async_copy(biases.at[0], gb.at[sec, 1], sem_w.at[3]),
    ]
    for c in own_w:
        c.start()
    barrier = pltpu.get_barrier_semaphore()

    def greet(i, _):
        pl.semaphore_signal(barrier, inc=1, device_id={"dp": lax.rem(me + i, n)}, device_id_type=MESH)
        return 0

    lax.fori_loop(1, n, greet, 0)
    pl.semaphore_signal(barrier, inc=1, device_id=partner, device_id_type=MESH)
    pl.semaphore_wait(barrier, n)
    send_w = [
        pltpu.make_async_remote_copy(kone.at[0], w1.at[sec], sem_ws.at[0], sem_wr.at[0], device_id=partner, device_id_type=MESH),
        pltpu.make_async_remote_copy(gains.at[0], gb.at[sec, 0], sem_ws.at[2], sem_wr.at[2], device_id=partner, device_id_type=MESH),
        pltpu.make_async_remote_copy(biases.at[0], gb.at[sec, 1], sem_ws.at[3], sem_wr.at[3], device_id=partner, device_id_type=MESH),
        pltpu.make_async_remote_copy(ktwo.at[0], w2.at[sec], sem_ws.at[1], sem_wr.at[1], device_id=partner, device_id_type=MESH),
    ]
    for c in send_w:
        c.start()

    def peers(ship):
        if n <= 16 and n & (n - 1) == 0:
            bits = [lax.rem(me // 2**b, 2) for b in range(n.bit_length() - 1)]
            for i in range(n - 1, 0, -1):
                ship(sum((1 - bit if i >> b & 1 else bit) * 2**b for b, bit in enumerate(bits)))
        else:

            def one(i, _):
                ship(lax.rem(me + i, n))
                return 0

            lax.fori_loop(1, n, one, 0)

    count_in.wait()
    entry = lax.broadcasted_iota(jnp.int32, (TILE, C), 0)
    slot = lax.rem(entry, slots)
    cmsg[...] = jnp.zeros_like(cmsg)
    for m in range(micro):
        filled = jnp.logical_and(slot < filled_here[0, first + m], entry < STRIPS * slots)
        masks[m, 0] = filled.astype(F32)
        masks[m, 1] = jnp.logical_and(filled, entry < (STRIPS - 1) * slots).astype(F32)

        cmsg[pl.ds(m, 1), :] = jnp.full((1, 128), filled_here[0, first + m].astype(F32) * float(board * board), F32)
    cinbox[me] = cmsg[...]
    peers(
        lambda to: pltpu.make_async_remote_copy(
            cmsg, cinbox.at[me], sem_c.at[0], sem_c.at[1], device_id={"dp": to}, device_id_type=MESH
        ).start()
    )
    edge = jnp.zeros((6, TILE, C), BF16)

    def clear(m, _):
        for ref in (xs.at[0], xs.at[1], us.at[0], us.at[1]):
            ref[m, :, pl.ds(0, TILE), :] = edge
            ref[m, :, pl.ds((board + 1) * TILE, TILE), :] = edge
        return 0

    lax.fori_loop(0, micro, clear, 0)
    ds[:, pl.ds(0, TILE), :] = edge
    ds[:, pl.ds((board + 1) * TILE, TILE), :] = edge

    def clear_acc(t, _):
        for k in range(2):
            for j in range(2):
                acc[k, j, pl.ds(t * C, C), :] = jnp.zeros((C, C), F32)
        return 0

    lax.fori_loop(0, 9, clear_acc, 0)
    temp[...] = jnp.zeros_like(temp)
    gacc[...] = jnp.zeros_like(gacc)

    def mask_of(m, ai):
        return masks[m, 1 if ai == AI - 1 else 0][None]

    def tiles(v):
        return v.reshape(board, TILE, C)

    def flat(v):
        return v.reshape(BT, C)

    def put(ref, ai, value):
        ref[ai + 1, pl.ds(TILE, BT), :] = flat(value).astype(BF16)
        if ai == AI - 1:
            ref[0, pl.ds(TILE, BT), :] = flat(pltpu.roll(value, slots, 1)).astype(BF16)
        if ai == 0:
            ref[AI + 1, pl.ds(TILE, BT), :] = flat(pltpu.roll(value, TILE - slots, 1)).astype(BF16)

    def window(ref, ai, i, j):
        return ref[ai + i, pl.ds(j * TILE, BT), :]

    def inner(ref, ai):
        return window(ref, ai, 1, 1)

    def conv(ref, ai, weights):
        lhs = jnp.concatenate([window(ref, ai, i, j) for i in range(3) for j in range(3)], axis=1)
        return jnp.dot(lhs, weights[...].reshape(9 * C, C), preferred_element_type=F32)

    def conv_back(ref, ai, weights):
        out = None
        for i in range(3):
            for j in range(3):
                part = lax.dot_general(
                    window(ref, ai, i, j), weights[(2 - i) * 3 + 2 - j], (((1,), (1,)), ((), ())), preferred_element_type=F32
                )
                out = part if out is None else out + part
        return out

    def kernel_grad(total, pairs, taps=range(9)):
        lhs = jnp.concatenate([inner(ref, ai) for ref, _ in pairs for ai in range(AI)], axis=0)
        for t in taps:
            i, j = t // 3, t % 3
            rhs = jnp.concatenate([window(grad, ai, 2 - i, 2 - j) for _, grad in pairs for ai in range(AI)], axis=0)
            total[pl.ds(t * C, C), :] += lax.dot_general(lhs, rhs, (((0,), (0,)), ((), ())), preferred_element_type=F32)

    def fold(v):
        return jnp.sum(v.reshape(BT // 8, 8, C), axis=0)

    def send_stats(phase, m, one, two):
        par = phase % 2
        one = jnp.sum(one, axis=0, keepdims=True)
        two = jnp.sum(two, axis=0, keepdims=True)
        for r, v in enumerate((one[:, :128], one[:, 128:], two[:, :128], two[:, 128:])):
            msg[par, m, pl.ds(r, 1), :] = v
        inbox[par, m, me] = msg[par, m]
        peers(
            lambda to: pltpu.make_async_remote_copy(
                msg.at[par, m], inbox.at[par, m, me], sem_msg.at[par, m], sem_inbox.at[par, m],
                device_id={"dp": to}, device_id_type=MESH,
            ).start()
        )

    def get_stats(phase, m):
        par = phase % 2
        several = inbox.at[par, m, pl.ds(0, n - 1)]
        pltpu.make_async_copy(several, several, sem_inbox.at[par, m]).wait()
        pltpu.make_async_copy(several, several, sem_msg.at[par, m]).wait()
        if n <= 16:
            total = inbox[par, m, 0]
            for d in range(1, n):
                total = total + inbox[par, m, d]
        else:
            total = jnp.sum(inbox[par, m], axis=0)
        one = jnp.concatenate([total[0:1], total[1:2]], axis=1)
        two = jnp.concatenate([total[2:3], total[3:4]], axis=1)
        return one, two

    def norm_coefs(phase, m, k, j):
        one, two = get_stats(phase, m)
        count = jnp.concatenate([totals[pl.ds(m, 1), :]] * (C // 128), axis=1)
        mean = one / count
        var = two / count - mean * mean
        r = lax.rsqrt(var + 1e-5)
        scale = r * gb[k, 0, pl.ds(j, 1), :]
        offset = gb[k, 1, pl.ds(j, 1), :] - mean * scale
        for q, v in enumerate((0.5 * scale, 0.5 * offset, r, mean, count, scale)):
            coef[k, j, m, pl.ds(q, 1), :] = v
        return 0.5 * scale, 0.5 * offset

    def kept(m, k, j):
        return coef[k, j, m, pl.ds(0, 1), :], coef[k, j, m, pl.ds(1, 1), :]

    def back_coefs(phase, m, k, j):
        sdy, sdh = get_stats(phase, m)
        r, mean = coef[k, j, m, pl.ds(2, 1), :], coef[k, j, m, pl.ds(3, 1), :]
        count, alpha = coef[k, j, m, pl.ds(4, 1), :], coef[k, j, m, pl.ds(5, 1), :]
        sdx = r * (sdh - mean * sdy)
        gacc[k, 0, pl.ds(j, 1), :] += sdx
        gacc[k, 1, pl.ds(j, 1), :] += sdy
        gamma = -alpha * r * sdx / count
        beta = -alpha * sdy / count - gamma * mean
        return alpha, gamma, beta

    def silu2(z):
        return z + z * jnp.tanh(z)

    def slope2(z):
        t = jnp.tanh(z)
        return (0.5 + 0.5 * t) * (1.0 + z * (1.0 - t))

    def places():
        return [(p, a) for p in range(slots) for a in range(board)]

    def spread(m):
        for p, a in places():
            rows = pl.ds(a // AI * slots + p, board, TILE)
            for c in range(C // 128):
                temp[c, a % AI, rows, :] = stage[m, p, a, :, pl.ds(128 * c, 128)].astype(F32)

    def gather(m):
        for p, a in places():
            rows = pl.ds(a // AI * slots + p, board, TILE)
            for c in range(C // 128):
                ostage[lax.rem(m, 2), p, a, :, pl.ds(128 * c, 128)] = temp[c, a % AI, rows, :].astype(BF16)

    def read_temp(ai):
        return jnp.concatenate([temp[c, ai] for c in range(C // 128)], axis=1)

    def write_temp(ai, v):
        for c in range(C // 128):
            temp[c, ai] = v[:, 128 * c : 128 * (c + 1)]

    def wait_out(m):
        o = lax.rem(m, 2)
        pltpu.make_async_copy(ostage.at[o], ostage.at[o], sem_out.at[o]).wait()

    def emit(which, k, m):
        out = (hidden, igrads)[which]
        o = lax.rem(m, 2)

        @pl.when(sec == k)
        def _():
            pltpu.make_async_copy(ostage.at[o], out.at[0, first + m], sem_out.at[o]).start()

        @pl.when(sec != k)
        def _():
            pltpu.make_async_remote_copy(
                ostage.at[o], out.at[0, first + m], sem_out.at[o], sem_outr.at[which, m], device_id=partner, device_id_type=MESH
            ).start()

    def each(body):
        def step(m, _):
            body(m)
            return 0

        lax.fori_loop(0, micro, step, 0)

    def run_conv(phase, m, ref, weights, target):
        one = two = jnp.zeros((8, C), F32)
        for ai in range(AI):
            h = conv(ref, ai, weights)
            target[ai] = h
            if ai == AI - 1:
                h = flat(tiles(h) * mask_of(m, ai))
            one = one + fold(h)
            two = two + fold(h * h)
        send_stats(phase, m, one, two)

    ORDER = (AI - 1,) + tuple(range(AI - 1))

    def first_conv(m):
        pltpu.make_async_copy(stage.at[m], stage.at[m], sem_in.at[m]).wait()
        spread(m)
        pltpu.make_async_copy(cot.at[first + m], stage.at[m], sem_cot.at[m]).start()
        for ai in ORDER:
            put(xs.at[0, m], ai, tiles(read_temp(ai)) * mask_of(m, ai))
        run_conv(0, m, xs.at[0, m], w1.at[0], h1.at[0, m])

    def second_conv(phase, k):
        def body(m):
            a, b = norm_coefs(phase - 1, m, k, 0)
            for ai in ORDER:
                put(us.at[k, m], ai, tiles(silu2(h1[k, m, ai] * a + b)) * mask_of(m, ai))
            run_conv(phase, m, us.at[k, m], w2.at[k], h2.at[k, m])

        return body

    def third_conv(m):
        @pl.when(m >= 2)
        def _():
            wait_out(m)

        a, b = norm_coefs(1, m, 0, 1)
        for ai in ORDER:
            z = h2[0, m, ai] * a + b + 0.5 * inner(xs.at[0, m], ai).astype(F32)
            x = tiles(silu2(z)) * mask_of(m, ai)
            put(xs.at[1, m], ai, x)
            write_temp(ai, flat(x))
        run_conv(2, m, xs.at[1, m], w1.at[1], h1.at[1, m])
        gather(m)
        emit(0, 0, m)

    def turn(m):
        a, b = norm_coefs(3, m, 1, 1)
        wait_out(m)
        for ai in range(AI):
            z = h2[1, m, ai] * a + b + 0.5 * inner(xs.at[1, m], ai).astype(F32)
            write_temp(ai, flat(tiles(silu2(z)) * mask_of(m, ai)))
        gather(m)
        emit(0, 1, m)
        pltpu.make_async_copy(stage.at[m], stage.at[m], sem_cot.at[m]).wait()
        write_temp(AI - 1, jnp.zeros((BT, C), F32))
        spread(m)
        one = two = jnp.zeros((8, C), F32)
        for ai in range(AI):
            h = h2[1, m, ai]
            z = h * a + b + 0.5 * inner(xs.at[1, m], ai).astype(F32)
            dy = flat(tiles(read_temp(ai) * slope2(z)) * mask_of(m, ai))
            dp_[m, ai] = dy
            one = one + fold(dy)
            two = two + fold(dy * h)
        send_stats(4, m, one, two)

    def second_grad(phase, k, m, grad):
        alpha, gamma, beta = back_coefs(phase - 1, m, k, 1)
        for ai in ORDER:
            put(grad, ai, tiles(alpha * dp_[m, ai] + gamma * h2[k, m, ai] + beta) * mask_of(m, ai))
        a, b = kept(m, k, 0)
        one = two = jnp.zeros((8, C), F32)
        for ai in range(AI):
            du = conv_back(grad, ai, w2.at[k])
            h = h1[k, m, ai]
            dy = du * slope2(h * a + b)
            if ai == AI - 1:
                dy = flat(tiles(dy) * mask_of(m, ai))
            dy_[m, ai] = dy
            one = one + fold(dy)
            two = two + fold(dy * h)
        send_stats(phase, m, one, two)

    def first_prep(phase, k, m, grad):
        alpha, gamma, beta = back_coefs(phase - 1, m, k, 0)
        for ai in ORDER:
            put(grad, ai, tiles(alpha * dy_[m, ai] + gamma * h1[k, m, ai] + beta) * mask_of(m, ai))

    def first_grad(phase, k, m, grad):
        wait_out(m)
        if k == 1:
            a, b = kept(m, 0, 1)
            one = two = jnp.zeros((8, C), F32)
        for ai in range(AI):
            dx = (conv_back(grad, ai, w1.at[k]) + dp_[m, ai]).astype(BF16).astype(F32)
            write_temp(ai, dx)
            if k == 1:
                h = h2[0, m, ai]
                z = h * a + b + 0.5 * inner(xs.at[0, m], ai).astype(F32)
                dy = dx * slope2(z)
                if ai == AI - 1:
                    dy = flat(tiles(dy) * mask_of(m, ai))
                dp_[m, ai] = dy
                one = one + fold(dy)
                two = two + fold(dy * h)
        if k == 1:
            send_stats(phase, m, one, two)
        gather(m)
        emit(1, k, m)

    R = g.rows
    HALF, QUARTER, SHARD = R // 2, R // 4, R // 4 // g.deep
    bit0, bit1 = lax.rem(me, 2), lax.rem(me // 2, 2)
    deep_at = lax.rem(me // 4, g.deep)
    rep_at = me // (4 * g.deep)
    near = ({"dp": me + 1 - 2 * bit0}, {"dp": me + 2 - 4 * bit1})
    order = ((bit0, bit1), (bit1, bit0))

    def rows(start, size):
        return pl.ds(pl.multiple_of(start, 16), size)

    def columns(h):
        return pl.ds(128 * h, 128)

    def remote(src, dst, job, step, to):
        pltpu.make_async_remote_copy(src, dst, sem_js.at[job, step], sem_jr.at[job, step], device_id=to, device_id_type=MESH).start()

    def arrived(ref, job, step):
        pltpu.make_async_copy(ref, ref, sem_jr.at[job, step]).wait()

    def left(ref, job, step):
        pltpu.make_async_copy(ref, ref, sem_js.at[job, step]).wait()

    def deep_peers():
        for i in range(1, g.deep):
            t = lax.rem(deep_at + i, g.deep)
            yield t, {"dp": me + (t - deep_at) * 4}

    def rep_peers():
        for i in range(1, g.reps):
            t = lax.rem(rep_at + i, g.reps)
            yield t, {"dp": me + (t - rep_at) * 4 * g.deep}

    def job_steps(k, j, c):
        base = c * R
        q = j * g.parts + c
        total = acc.at[k, j]
        start1 = [order[h][0] * HALF for h in range(2)]
        start2 = [start1[h] + order[h][1] * QUARTER for h in range(2)]
        start3 = [start2[h] + deep_at * SHARD for h in range(2)]

        def give():
            if j == 0:
                left(psend.at[c], g.parts + c, 0)
                pl.semaphore_wait(sem_free.at[c], 1)
            for h in range(2):
                psend[c, h] = total[pl.ds(base, R), columns(h)].astype(BF16)
            remote(psend.at[c], precv.at[c], q, 0, partner)

        def step1():
            arrived(precv.at[c], q, 0)
            for h in range(2):
                away = (1 - order[h][0]) * HALF
                xsend[q, h] = (total[rows(base + away, HALF), columns(h)] + precv[c, h, rows(away, HALF), :].astype(F32)).astype(BF16)
                remote(xsend.at[q, h], xrecv.at[q, h], q, 1, near[h])
            for h in range(2):
                total[rows(base + start1[h], HALF), columns(h)] += precv[c, h, rows(start1[h], HALF), :].astype(F32)
            if j == 1:
                pl.semaphore_signal(sem_free.at[c], inc=1, device_id=partner, device_id_type=MESH)

        def step2():
            arrived(xrecv.at[q], q, 1)
            for h in range(2):
                away = (1 - order[h][1]) * QUARTER
                ysend[q, h] = (
                    total[rows(base + start1[h] + away, QUARTER), columns(h)] + xrecv[q, h, rows(away, QUARTER), :].astype(F32)
                ).astype(BF16)
                remote(ysend.at[q, h], yrecv.at[q, h], q, 2, near[1 - h])
            for h in range(2):
                keep = order[h][1] * QUARTER
                total[rows(base + start2[h], QUARTER), columns(h)] += xrecv[q, h, rows(keep, QUARTER), :].astype(F32)

        def step3():
            arrived(yrecv.at[q], q, 2)
            for h in range(2):
                v = total[rows(base + start2[h], QUARTER), columns(h)] + yrecv[q, h].astype(F32)
                total[rows(base + start2[h], QUARTER), columns(h)] = v
                v = v.astype(BF16)
                for t in range(g.deep):
                    zsend[q, t, h] = v[t * SHARD : (t + 1) * SHARD]
            for t, to in deep_peers():
                remote(zsend.at[q, t], zrecv.at[q, deep_at], q, 3, to)

        def summed(h):
            v = total[rows(base + start3[h], SHARD), columns(h)]
            for t, _ in deep_peers():
                v = v + zrecv[q, t, h].astype(F32)
            return v

        def spread_deep():
            for h in range(2):
                mine = result.at[q, h, rows(start3[h], SHARD)]
                for _, to in deep_peers():
                    remote(mine, mine, q, 4, to)

        def step4():
            arrived(zrecv.at[q, pl.ds(0, g.deep - 1)], q, 3)
            for h in range(2):
                v = summed(h)
                if g.reps == 1:
                    result[q, h, rows(start3[h], SHARD), :] = v.astype(BF16)
                else:
                    total[rows(base + start3[h], SHARD), columns(h)] = v
                    zsend[q, deep_at, h] = v.astype(BF16)
            if g.reps == 1:
                spread_deep()
            else:
                for t, to in rep_peers():
                    remote(zsend.at[q, deep_at], rrecv.at[q, rep_at], q, 7, to)

        def step4_more():
            arrived(rrecv.at[q, pl.ds(0, g.reps - 1)], q, 7)
            for h in range(2):
                v = total[rows(base + start3[h], SHARD), columns(h)]
                for t, _ in rep_peers():
                    v = v + rrecv[q, t, h].astype(F32)
                result[q, h, rows(start3[h], SHARD), :] = v.astype(BF16)
            spread_deep()

        def step5():
            arrived(zrecv.at[q, pl.ds(0, g.deep - 1)], q, 4)
            for h in range(2):
                mine = result.at[q, h, rows(start2[h], QUARTER)]
                remote(mine, mine, q, 5, near[1 - h])

        def step6():
            arrived(yrecv.at[q], q, 5)
            for h in range(2):
                mine = result.at[q, h, rows(start1[h], HALF)]
                remote(mine, mine, q, 6, near[h])

        def step7():
            arrived(xrecv.at[q], q, 6)
            kout = (kout1, kout2)[j]
            for h in range(2):
                pltpu.make_async_copy(result.at[q, h], kout.at[h, pl.ds(base, R), :], sem_res.at[q, h]).start()

        def done():
            for h in range(2):
                pltpu.make_async_copy(result.at[q, h], result.at[q, h], sem_res.at[q, h]).wait()
            left(xsend.at[q], q, 1)
            left(ysend.at[q], q, 2)
            left(zsend.at[q, pl.ds(0, g.deep - 1)], q, 3)
            left(zsend.at[q, pl.ds(0, g.deep - 1)], q, 4)
            left(ysend.at[q], q, 5)
            left(xsend.at[q], q, 6)
            if g.reps > 1:
                left(rrecv.at[q, pl.ds(0, g.reps - 1)], q, 7)

        middle = [step4] if g.reps == 1 else [step4, step4_more]
        return give, [step1, step2, step3] + middle + [step5, step6, step7], done

    clock, link = [0.0], [0.0]
    open_jobs, finals = [], []
    LATENCY = g.latency

    def begin(k, j, c):
        give, steps, done = job_steps(k, j, c)
        pl.when(sec != k)(give)
        link_core = clock[0] + LATENCY[0]
        open_jobs.append([link_core, k, steps, 0])
        finals.append((k, done))

    def advance(spent):
        clock[0] += spent
        ready = sorted((job for job in open_jobs if job[0] <= clock[0]), key=lambda job: job[0])
        for job in ready:
            run_step(job)

    def run_step(job):
        _, k, steps, at = job
        pl.when(sec == k)(steps[at])
        at += 1
        if at == len(steps):
            open_jobs.remove(job)
            return
        use, wait = LATENCY[at]
        link[0] = max(link[0], clock[0]) + use
        job[0], job[3] = link[0] + wait, at

    def drain():
        while open_jobs:
            job = min(open_jobs, key=lambda job: job[0])
            clock[0] = max(clock[0], job[0])
            run_step(job)

    @pl.when(sec == 0)
    def _():
        own_w[0].wait()

    @pl.when(sec != 0)
    def _():
        pltpu.make_async_copy(w1.at[other], w1.at[other], sem_wr.at[0]).wait()

    each(first_conv)
    several = cinbox.at[pl.ds(0, n - 1)]
    pltpu.make_async_copy(several, several, sem_c.at[1]).wait()
    pltpu.make_async_copy(several, several, sem_c.at[0]).wait()
    totals[...] = jnp.sum(cinbox[...], axis=0)
    for c in own_w[1:]:
        c.wait()

    @pl.when(sec != 0)
    def _():
        own_w[0].wait()

    for ref, q in ((w2.at[other], 1), (gb.at[other, 0], 2), (gb.at[other, 1], 3)):
        pltpu.make_async_copy(ref, ref, sem_wr.at[q]).wait()

    each(second_conv(1, 0))

    @pl.when(sec == 0)
    def _():
        pltpu.make_async_copy(w1.at[other], w1.at[other], sem_wr.at[0]).wait()

    for c in send_w:
        c.wait_send()
    each(third_conv)
    each(second_conv(3, 1))
    each(turn)

    def both(m):
        second_grad(5, 1, m, ds)
        kernel_grad(acc.at[1, 1], [(us.at[1, m], ds)])

    each(both)
    everyone = range(micro)
    for c in range(g.parts):
        begin(1, 1, c)
    for m in everyone:
        first_prep(6, 1, m, ds)
        first_grad(6, 1, m, ds)
        advance(2.3)
        kernel_grad(acc.at[1, 0], [(xs.at[1, m], ds)])
        advance(1.75)
    for c in range(g.parts):
        begin(1, 0, c)
    for m in everyone:
        second_grad(7, 0, m, us.at[1, m])
        advance(1.9)
    taps = 9 // g.parts
    for c in range(g.parts):
        kernel_grad(acc.at[0, 1], [(us.at[0, m], us.at[1, m]) for m in everyone], range(c * taps, (c + 1) * taps))
        begin(0, 1, c)
        advance(1.75)
    for m in everyone:
        first_prep(8, 0, m, xs.at[1, m])
        advance(0.4)
    for c in range(g.parts):
        kernel_grad(acc.at[0, 0], [(xs.at[0, m], xs.at[1, m]) for m in everyone], range(c * taps, (c + 1) * taps))
        begin(0, 0, c)
        advance(1.75)
    for m in everyone:
        first_grad(8, 0, m, xs.at[1, m])
        advance(1.9)

    swap = pltpu.make_async_remote_copy(gacc.at[other], grecv, sem_g.at[0], sem_g.at[1], device_id=partner, device_id_type=MESH)
    swap.start()
    drain()
    swap.wait()
    gout[0] = gacc[sec, 0] + grecv[0]
    bout[0] = gacc[sec, 1] + grecv[1]
    for m in range(1, micro):
        wait_out(m)
    for which, out in enumerate((hidden, igrads)):
        for m in range(micro):
            came = out.at[0, other * micro + m]
            pltpu.make_async_copy(came, came, sem_outr.at[which, m]).wait()
    for c in range(g.parts):
        left(psend.at[c], c, 0)
    for k, done in finals:
        pl.when(sec == k)(done)


def local(n, boards, cotangent, counts, kernel_one, kernel_two, gains, biases):
    g = Plan()
    micro, slots, board, _, C = boards.shape
    g.n, g.half, g.slots, g.board, g.channels = n, micro // 2, slots, board, C
    half = g.half
    BT = board * TILE
    haloed = (AI + 2, (board + 2) * TILE, C)
    dense = (AI, BT, C)
    flat_kernel = (1, 9, C, C)
    g.parts = 3
    g.rows = 9 * C // g.parts
    g.deep = 4 if n % 16 == 0 else 1
    g.reps = n // (4 * g.deep)
    jobs = 2 * g.parts
    R = g.rows
    shard = R // 4 // g.deep
    g.latency = [2.7, (0.7, 1.8), (0.4, 1.8), (0.7, 2.1), (0.7, 2.1), (0.4, 1.8), (0.7, 1.8), (0.0, 0.0), (0.0, 0.0)]
    dma = pltpu.SemaphoreType.DMA
    scratch = [
        pltpu.VMEM((half, slots, board, board, C), BF16),
        pltpu.VMEM((2, slots, board, board, C), BF16),
        pltpu.VMEM((C // 128, AI, BT, 128), F32),
        pltpu.VMEM((2, half) + haloed, BF16),
        pltpu.VMEM((2, half) + haloed, BF16),
        pltpu.VMEM(haloed, BF16),
        pltpu.VMEM((2, half) + dense, F32),
        pltpu.VMEM((2, half) + dense, F32),
        pltpu.VMEM((half,) + dense, F32),
        pltpu.VMEM((2, 9, C, C), BF16),
        pltpu.VMEM((2, 9, C, C), BF16),
        pltpu.VMEM((2, 2, 2, C), F32),
        pltpu.VMEM((2, 2, half, 8, C), F32),
        pltpu.VMEM((half, 2, TILE, C), F32),
        pltpu.VMEM((2, 2, 9 * C, C), F32),
        pltpu.VMEM((2, half, 4, 128), F32),
        pltpu.VMEM((2, half, n, 4, 128), F32),
        pltpu.VMEM((4, 128), F32),
        pltpu.VMEM((n, 4, 128), F32),
        pltpu.VMEM((4, 128), F32),
        pltpu.VMEM((2, 2, 2, C), F32),
        pltpu.VMEM((2, 2, C), F32),
        pltpu.SMEM((1, micro), jnp.int32),
        pltpu.VMEM((g.parts, 2, R, 128), BF16),
        pltpu.VMEM((g.parts, 2, R, 128), BF16),
        pltpu.VMEM((jobs, 2, R // 2, 128), BF16),
        pltpu.VMEM((jobs, 2, R // 2, 128), BF16),
        pltpu.VMEM((jobs, 2, R // 4, 128), BF16),
        pltpu.VMEM((jobs, 2, R // 4, 128), BF16),
        pltpu.VMEM((jobs, g.deep, 2, shard, 128), BF16),
        pltpu.VMEM((jobs, g.deep, 2, shard, 128), BF16),
        pltpu.VMEM((jobs, g.reps, 2, shard, 128) if g.reps > 1 else (1, 16, 128), BF16),
        pltpu.VMEM((jobs, 2, R, 128), BF16),
        dma((half,)), dma((half,)), dma((5,)), dma((4,)), dma((4,)),
        dma((2,)), dma((2, half)), dma((2, half)), dma((2, half)), dma((2,)), dma((2,)), dma((jobs, 8)), dma((jobs, 8)), dma((jobs, 2)),
        pltpu.SemaphoreType.REGULAR((g.parts,)),
    ]
    anywhere = pl.BlockSpec(memory_space=pl.ANY)
    vmem = pl.BlockSpec(memory_space=pltpu.VMEM)
    field = jax.ShapeDtypeStruct((1,) + boards.shape, BF16)
    grad = jax.ShapeDtypeStruct((2, 9 * C, 128), BF16)
    pair = jax.ShapeDtypeStruct(gains.shape, F32)
    hidden, igrads, k1, k2, gg, bg = pl.pallas_call(
        functools.partial(kernel, g),
        out_shape=(field, field, grad, grad, pair, pair),
        in_specs=[anywhere] * 7,
        out_specs=(anywhere, anywhere, anywhere, anywhere, vmem, vmem),
        scratch_shapes=scratch,
        compiler_params=pltpu.CompilerParams(collective_id=0, has_side_effects=True, vmem_limit_bytes=(63 * 16 + 14) * 2**16),
    )(
        boards, cotangent, counts.T, kernel_one.reshape(flat_kernel), kernel_two.reshape(flat_kernel), gains, biases
    )

    def widen(k):
        return jnp.concatenate([k[0], k[1]], axis=1).astype(F32).reshape(kernel_one.shape)

    return hidden, igrads, widen(k1), widen(k2), gg, bg


def solution(mesh):
    return jax.shard_map(
        functools.partial(local, mesh.shape["dp"]),
        mesh=mesh,
        in_specs=(
            P(None, "dp", None, None, None),
            P(None, "dp", None, None, None),
            P(None, "dp"),
            P("section", None, None, None, None),
            P("section", None, None, None, None),
            P("section", None, None),
            P("section", None, None),
        ),
        out_specs=(
            P("section", None, "dp", None, None, None),
            P("section", None, "dp", None, None, None),
            P("section", None, None, None, None),
            P("section", None, None, None, None),
            P("section", None, None),
            P("section", None, None),
        ),
        check_vma=False,
    )
```

```python
import functools

import jax
import jax.numpy as jnp
from jax import lax
from jax.experimental import pallas as pl
from jax.experimental.pallas import tpu as pltpu
from jax.sharding import PartitionSpec as P

MESH = pl.DeviceIdType.MESH
F32, BF16 = jnp.float32, jnp.bfloat16

STRIPS, AI, TILE = 5, 4, 16


class Plan:
    pass


def kernel(g, *refs):
    (
        boards, cot, counts, kone, ktwo, gains, biases,
        hidden, igrads, kout1, kout2, gout, bout,
        stage, ostage, temp, xs, us, ds, h1, h2, dp_, w1, w2, gb, coef, masks, acc, msg, inbox, cmsg, cinbox, totals, gacc, grecv, filled_here,
        psend, precv, xsend, xrecv, ysend, yrecv, zsend, zrecv, rrecv, result,
        sem_in, sem_cot, sem_w, sem_wr, sem_ws, sem_out, sem_outs, sem_outr, sem_msg, sem_inbox, sem_c, sem_g, sem_js, sem_jr, sem_res, sem_free,
    ) = refs
    dy_ = h2.at[1]
    n, micro, slots, board, C = g.n, g.half, g.slots, g.board, g.channels
    BT = board * TILE
    me = lax.axis_index("dp")
    sec = lax.axis_index("section")
    other = 1 - sec
    partner = {"section": other}
    first = sec * micro

    def load_in(src, m, slot, sem):
        return pltpu.make_async_copy(src.at[first + m], stage.at[slot], sem.at[m])

    barrier = pltpu.get_barrier_semaphore()

    def greet(i, _):
        pl.semaphore_signal(barrier, inc=1, device_id={"dp": lax.rem(me + i, n)}, device_id_type=MESH)
        return 0

    pl.semaphore_signal(barrier, inc=1, device_id=partner, device_id_type=MESH)
    lax.fori_loop(1, n, greet, 0, unroll=n <= 16)
    count_in = pltpu.make_async_copy(counts, filled_here, sem_w.at[4])
    count_in.start()
    for m in range(2):
        load_in(boards, m, m, sem_in).start()
    own_w = [
        pltpu.make_async_copy(kone.at[0], w1.at[sec], sem_w.at[0]),
        pltpu.make_async_copy(ktwo.at[0], w2.at[sec], sem_w.at[1]),
        pltpu.make_async_copy(gains.at[0], gb.at[sec, 0], sem_w.at[2]),
        pltpu.make_async_copy(biases.at[0], gb.at[sec, 1], sem_w.at[3]),
    ]
    for c in own_w:
        c.start()
    pl.semaphore_wait(barrier, n)
    send_w = [
        pltpu.make_async_remote_copy(kone.at[0], w1.at[sec], sem_ws.at[0], sem_wr.at[0], device_id=partner, device_id_type=MESH),
        pltpu.make_async_remote_copy(gains.at[0], gb.at[sec, 0], sem_ws.at[2], sem_wr.at[2], device_id=partner, device_id_type=MESH),
        pltpu.make_async_remote_copy(biases.at[0], gb.at[sec, 1], sem_ws.at[3], sem_wr.at[3], device_id=partner, device_id_type=MESH),
        pltpu.make_async_remote_copy(ktwo.at[0], w2.at[sec], sem_ws.at[1], sem_wr.at[1], device_id=partner, device_id_type=MESH),
    ]
    for c in send_w:
        c.start()

    def peers(ship):
        if n <= 16 and n & (n - 1) == 0:
            bits = [lax.rem(me // 2**b, 2) for b in range(n.bit_length() - 1)]
            for i in range(n - 1, 0, -1):
                ship(sum((1 - bit if i >> b & 1 else bit) * 2**b for b, bit in enumerate(bits)))
        else:

            def one(i, _):
                ship(lax.rem(me + i, n))
                return 0

            lax.fori_loop(1, n, one, 0)

    count_in.wait()
    entry = lax.broadcasted_iota(jnp.int32, (TILE, C), 0)
    slot = lax.rem(entry, slots)
    cmsg[...] = jnp.zeros_like(cmsg)
    for m in range(micro):
        filled = jnp.logical_and(slot < filled_here[0, first + m], entry < STRIPS * slots)
        masks[m, 0] = filled.astype(F32)
        masks[m, 1] = jnp.logical_and(filled, entry < (STRIPS - 1) * slots).astype(F32)

        cmsg[pl.ds(m, 1), :] = jnp.full((1, 128), filled_here[0, first + m].astype(F32) * float(board * board), F32)
    cinbox[me] = cmsg[...]
    peers(
        lambda to: pltpu.make_async_remote_copy(
            cmsg, cinbox.at[me], sem_c.at[0], sem_c.at[1], device_id={"dp": to}, device_id_type=MESH
        ).start()
    )
    edge = jnp.zeros((6, TILE, C), BF16)

    def clear(m, _):
        for ref in (xs.at[0], xs.at[1], us.at[0], us.at[1]):
            ref[m, :, pl.ds(0, TILE), :] = edge
            ref[m, :, pl.ds((board + 1) * TILE, TILE), :] = edge
        return 0

    lax.fori_loop(0, micro, clear, 0)
    for q in range(2):
        ds[q, :, pl.ds(0, TILE), :] = edge
        ds[q, :, pl.ds((board + 1) * TILE, TILE), :] = edge
    temp[...] = jnp.zeros_like(temp)
    dp_[...] = jnp.zeros_like(dp_)
    gacc[...] = jnp.zeros_like(gacc)

    def mask_of(m, ai):
        return masks[m, 1 if ai == AI - 1 else 0][None]

    def tiles(v):
        return v.reshape(board, TILE, C)

    def flat(v):
        return v.reshape(BT, C)

    def put(ref, ai, value):
        ref[ai + 1, pl.ds(TILE, BT), :] = flat(value).astype(BF16)
        if ai == AI - 1:
            ref[0, pl.ds(TILE, BT), :] = flat(pltpu.roll(value, slots, 1)).astype(BF16)
        if ai == 0:
            ref[AI + 1, pl.ds(TILE, BT), :] = flat(pltpu.roll(value, TILE - slots, 1)).astype(BF16)

    def window(ref, ai, i, j):
        return ref[ai + i, pl.ds(j * TILE, BT), :]

    def inner(ref, ai):
        return window(ref, ai, 1, 1)

    def conv(ref, ai, weights):
        lhs = jnp.concatenate([window(ref, ai, i, j) for i in range(3) for j in range(3)], axis=1)
        return jnp.dot(lhs, weights[...].reshape(9 * C, C), preferred_element_type=F32)

    def conv_back(ref, ai, weights):
        out = None
        for i in range(3):
            for j in range(3):
                part = lax.dot_general(
                    window(ref, ai, i, j), weights[(2 - i) * 3 + 2 - j], (((1,), (1,)), ((), ())), preferred_element_type=F32
                )
                out = part if out is None else out + part
        return out

    def kernel_grad(total, pairs, taps=range(9), add=False):
        lhs = jnp.concatenate([inner(ref, ai) for ref, _ in pairs for ai in range(AI)], axis=0)
        for t in taps:
            i, j = t // 3, t % 3
            rhs = jnp.concatenate([window(grad, ai, 2 - i, 2 - j) for _, grad in pairs for ai in range(AI)], axis=0)
            d = lax.dot_general(lhs, rhs, (((0,), (0,)), ((), ())), preferred_element_type=F32)
            for h in range(2):
                at, part = (h, pl.ds(t * C, C)), d[:, 128 * h : 128 * (h + 1)]
                total[at] = total[at] + part if add else part

    def fold(v):
        return jnp.sum(v.reshape(BT // 8, 8, C), axis=0)

    def send_stats(phase, m, one, two):
        par = phase % 2
        one = jnp.sum(one, axis=0, keepdims=True)
        two = jnp.sum(two, axis=0, keepdims=True)
        for r, v in enumerate((one[:, :128], one[:, 128:], two[:, :128], two[:, 128:])):
            msg[par, m, pl.ds(r, 1), :] = v
        inbox[par, m, me] = msg[par, m]
        peers(
            lambda to: pltpu.make_async_remote_copy(
                msg.at[par, m], inbox.at[par, m, me], sem_msg.at[par, m], sem_inbox.at[par, m],
                device_id={"dp": to}, device_id_type=MESH,
            ).start()
        )

    def get_stats(phase, m):
        par = phase % 2
        several = inbox.at[par, m, pl.ds(0, n - 1)]
        pltpu.make_async_copy(several, several, sem_inbox.at[par, m]).wait()
        pltpu.make_async_copy(several, several, sem_msg.at[par, m]).wait()
        if n <= 16:
            total = inbox[par, m, 0]
            for d in range(1, n):
                total = total + inbox[par, m, d]
        else:
            total = jnp.sum(inbox[par, m], axis=0)
        one = jnp.concatenate([total[0:1], total[1:2]], axis=1)
        two = jnp.concatenate([total[2:3], total[3:4]], axis=1)
        return one, two

    def norm_coefs(phase, m, k, j):
        one, two = get_stats(phase, m)
        count = jnp.concatenate([totals[pl.ds(m, 1), :]] * (C // 128), axis=1)
        mean = one / count
        var = two / count - mean * mean
        r = lax.rsqrt(var + 1e-5)
        scale = r * gb[k, 0, pl.ds(j, 1), :]
        offset = gb[k, 1, pl.ds(j, 1), :] - mean * scale
        for q, v in enumerate((0.5 * scale, 0.5 * offset, r, mean, count, scale)):
            coef[k, j, m, pl.ds(q, 1), :] = v
        return 0.5 * scale, 0.5 * offset

    def kept(m, k, j):
        return coef[k, j, m, pl.ds(0, 1), :], coef[k, j, m, pl.ds(1, 1), :]

    def back_coefs(phase, m, k, j):
        sdy, sdh = get_stats(phase, m)
        r, mean = coef[k, j, m, pl.ds(2, 1), :], coef[k, j, m, pl.ds(3, 1), :]
        count, alpha = coef[k, j, m, pl.ds(4, 1), :], coef[k, j, m, pl.ds(5, 1), :]
        sdx = r * (sdh - mean * sdy)
        gacc[k, 0, pl.ds(j, 1), :] += sdx
        gacc[k, 1, pl.ds(j, 1), :] += sdy
        gamma = -alpha * r * sdx / count
        beta = -alpha * sdy / count - gamma * mean
        return alpha, gamma, beta

    def silu2(z):
        return z + z * jnp.tanh(z)

    def slope2(z):
        t = jnp.tanh(z)
        return (0.5 + 0.5 * t) * (1.0 + z * (1.0 - t))

    def places():
        return [(p, a) for p in range(slots) for a in range(board)]

    def spread(slot, to):
        for p, a in places():
            rows = pl.ds(a // AI * slots + p, board, TILE)
            for c in range(C // 128):
                to[c, a % AI, rows, :] = stage[slot, p, a, :, pl.ds(128 * c, 128)].astype(F32)

    def gather(m, source):
        for p, a in places():
            rows = pl.ds(a // AI * slots + p, board, TILE)
            for c in range(C // 128):
                ostage[lax.rem(m, 2), p, a, :, pl.ds(128 * c, 128)] = source[c, a % AI, rows, :].astype(BF16)

    def read_split(ref, ai):
        return jnp.concatenate([ref[c, ai] for c in range(C // 128)], axis=1)

    def write_split(ref, ai, v):
        for c in range(C // 128):
            ref[c, ai] = v[:, 128 * c : 128 * (c + 1)]

    def wait_out(at):
        o = lax.rem(at, 2)
        for sems in (sem_out, sem_outs):
            pltpu.make_async_copy(ostage.at[o], ostage.at[o], sems.at[o]).wait()

    def emit(which, k, m, at=None):
        out = (hidden, igrads)[which]
        o = lax.rem(m if at is None else at, 2)
        away = lax.rem(sec + k, 2)
        pltpu.make_async_copy(ostage.at[o], out.at[away, first + m], sem_out.at[o]).start()
        pltpu.make_async_remote_copy(
            ostage.at[o], out.at[1 - away, first + m], sem_outs.at[o], sem_outr.at[which, k, m], device_id=partner, device_id_type=MESH
        ).start()

    def each(body):
        def step(m, _):
            body(m)
            return 0

        lax.fori_loop(0, micro, step, 0)

    def run_conv(phase, m, ref, weights, write):
        one = two = jnp.zeros((8, C), F32)
        for ai in range(AI):
            h = conv(ref, ai, weights)
            write(ai, h)
            if ai == AI - 1:
                h = flat(tiles(h) * mask_of(m, ai))
            one = one + fold(h)
            two = two + fold(h * h)
        send_stats(phase, m, one, two)

    ORDER = (AI - 1,) + tuple(range(AI - 1))

    def load_field(m, slot, following):
        load_in(boards, m, slot, sem_in).wait()
        spread(slot, temp)
        following.start()
        for ai in ORDER:
            put(xs.at[0, m], ai, tiles(read_split(temp, ai)) * mask_of(m, ai))

    def first_conv(m):
        run_conv(0, m, xs.at[0, m], w1.at[0], functools.partial(write_split, h1.at[0, m]))

    def second_conv(phase, k):
        def body(m):
            a, b = norm_coefs(phase - 1, m, k, 0)
            for ai in ORDER:
                put(us.at[k, m], ai, tiles(silu2(read_split(h1.at[k, m], ai) * a + b)) * mask_of(m, ai))

            def write(ai, h):
                h2[k, m, ai] = h

            run_conv(phase, m, us.at[k, m], w2.at[k], write)

        return body

    def third_conv(m):
        if m >= 2:
            wait_out(m)
        a, b = norm_coefs(1, m, 0, 1)
        for ai in ORDER:
            z = h2[0, m, ai] * a + b + 0.5 * inner(xs.at[0, m], ai).astype(F32)
            x = tiles(silu2(z)) * mask_of(m, ai)
            put(xs.at[1, m], ai, x)
            write_split(temp, ai, flat(x))
        run_conv(2, m, xs.at[1, m], w1.at[1], functools.partial(write_split, h1.at[1, m]))
        gather(m, temp)
        emit(0, 0, m)

    def turn(m):
        a, b = norm_coefs(3, m, 1, 1)
        one = two = jnp.zeros((8, C), F32)
        for ai in range(AI):
            h = h2[1, m, ai]
            z = h * a + b + 0.5 * inner(xs.at[1, m], ai).astype(F32)
            t = jnp.tanh(z)
            mask = mask_of(m, ai)
            write_split(temp, ai, flat(tiles(z + z * t) * mask))
            slope = (0.5 + 0.5 * t) * (1.0 + z * (1.0 - t))
            dy = flat(tiles(read_split(dp_.at[m], ai) * slope) * mask)
            write_split(dp_.at[m], ai, dy)
            one = one + fold(dy)
            two = two + fold(dy * h)
        send_stats(4, m, one, two)

    def second_prep(phase, k, m, grad):
        alpha, gamma, beta = back_coefs(phase - 1, m, k, 1)

        def go():
            for ai in ORDER:
                put(grad, ai, tiles(alpha * read_split(dp_.at[m], ai) + gamma * h2[k, m, ai] + beta) * mask_of(m, ai))

        return go

    def second_grad(phase, k, m, grad):
        a, b = kept(m, k, 0)
        one = two = jnp.zeros((8, C), F32)
        for ai in range(AI):
            du = conv_back(grad, ai, w2.at[k])
            h = read_split(h1.at[k, m], ai)
            dy = du * slope2(h * a + b)
            if ai == AI - 1:
                dy = flat(tiles(dy) * mask_of(m, ai))
            dy_[m, ai] = dy
            one = one + fold(dy)
            two = two + fold(dy * h)
        send_stats(phase, m, one, two)

    def first_prep(phase, k, m, grad):
        alpha, gamma, beta = back_coefs(phase - 1, m, k, 0)

        def go():
            for ai in ORDER:
                put(grad, ai, tiles(alpha * dy_[m, ai] + gamma * read_split(h1.at[k, m], ai) + beta) * mask_of(m, ai))

        return go

    def first_grad(phase, k, m, grad):
        if k == 1:
            a, b = kept(m, 0, 1)
            one = two = jnp.zeros((8, C), F32)
        for ai in range(AI):
            dx = (conv_back(grad, ai, w1.at[k]) + read_split(dp_.at[m], ai)).astype(BF16).astype(F32)
            write_split(h1.at[1, m] if k == 1 else temp, ai, dx)
            if k == 1:
                h = h2[0, m, ai]
                z = h * a + b + 0.5 * inner(xs.at[0, m], ai).astype(F32)
                dy = dx * slope2(z)
                if ai == AI - 1:
                    dy = flat(tiles(dy) * mask_of(m, ai))
                write_split(dp_.at[m], ai, dy)
                one = one + fold(dy)
                two = two + fold(dy * h)
        if k == 1:
            send_stats(phase, m, one, two)

    R = g.rows
    HALF, QUARTER, SHARD = R // 2, R // 4, R // 4 // g.deep
    bit0, bit1 = lax.rem(me, 2), lax.rem(me // 2, 2)
    deep_at = lax.rem(me // 4, g.deep)
    rep_at = me // (4 * g.deep)
    near = ({"dp": me + 1 - 2 * bit0}, {"dp": me + 2 - 4 * bit1})
    order = ((bit0, bit1), (bit1, bit0))

    def rows(start, size):
        return pl.ds(pl.multiple_of(start, 16), size)

    def remote(src, dst, job, step, to):
        pltpu.make_async_remote_copy(src, dst, sem_js.at[job, step], sem_jr.at[job, step], device_id=to, device_id_type=MESH).start()

    def arrived(ref, job, step):
        pltpu.make_async_copy(ref, ref, sem_jr.at[job, step]).wait()

    def left(ref, job, step):
        pltpu.make_async_copy(ref, ref, sem_js.at[job, step]).wait()

    def deep_peers():
        for i in range(1, g.deep):
            t = lax.rem(deep_at + i, g.deep)
            yield t, {"dp": me + (t - deep_at) * 4}

    def rep_peers():
        for i in range(1, g.reps):
            t = lax.rem(rep_at + i, g.reps)
            yield t, {"dp": me + (t - rep_at) * 4 * g.deep}

    def job_steps(k, j, first_part, number):
        parts = range(first_part, first_part + number)
        span = pl.ds(first_part, number)
        q0 = j * g.parts + first_part
        job = pl.ds(q0, number)
        total = acc.at[k, j]
        start1 = [order[h][0] * HALF for h in range(2)]
        start2 = [start1[h] + order[h][1] * QUARTER for h in range(2)]
        start3 = [start2[h] + deep_at * SHARD for h in range(2)]
        each_part = [(c, j * g.parts + c, c * R, h) for c in parts for h in range(2)]

        def give():
            if j == 0:
                for c in parts:
                    left(psend.at[c], c, 8)
                    pl.semaphore_wait(sem_free.at[c], 1)
            for c, q, base, h in each_part:
                psend[c, h] = total[h, pl.ds(base, R), :].astype(BF16)
            for c in parts:
                pltpu.make_async_remote_copy(
                    psend.at[c], precv.at[c], sem_js.at[c, 8 * j], sem_jr.at[j * g.parts + c, 0], device_id=partner, device_id_type=MESH
                ).start()

        def step1():
            for c, q, base, h in each_part:
                if h == 0:
                    arrived(precv.at[c], q, 0)
                away = (1 - order[h][0]) * HALF
                xsend[q, h] = (total[h, rows(base + away, HALF), :] + precv[c, h, rows(away, HALF), :].astype(F32)).astype(BF16)
            for h in range(2):
                remote(xsend.at[job, h], xrecv.at[job, h], q0, 1, near[h])
            for c, q, base, h in each_part:
                total[h, rows(base + start1[h], HALF), :] += precv[c, h, rows(start1[h], HALF), :].astype(F32)
            if j == 1:
                for c in parts:
                    pl.semaphore_signal(sem_free.at[c], inc=1, device_id=partner, device_id_type=MESH)

        def step2():
            arrived(xrecv.at[job], q0, 1)
            for c, q, base, h in each_part:
                away = (1 - order[h][1]) * QUARTER
                ysend[q, h] = (
                    total[h, rows(base + start1[h] + away, QUARTER), :] + xrecv[q, h, rows(away, QUARTER), :].astype(F32)
                ).astype(BF16)
            for h in range(2):
                remote(ysend.at[job, h], yrecv.at[job, h], q0, 2, near[1 - h])
            for c, q, base, h in each_part:
                keep = order[h][1] * QUARTER
                total[h, rows(base + start2[h], QUARTER), :] += xrecv[q, h, rows(keep, QUARTER), :].astype(F32)

        def step3():
            arrived(yrecv.at[job], q0, 2)
            for c, q, base, h in each_part:
                v = total[h, rows(base + start2[h], QUARTER), :] + yrecv[q, h].astype(F32)
                total[h, rows(base + start2[h], QUARTER), :] = v
                v = v.astype(BF16)
                for t in range(g.deep):
                    zsend[t, q, h] = v[t * SHARD : (t + 1) * SHARD]
            for t, to in deep_peers():
                remote(zsend.at[t, job], zrecv.at[deep_at, job], q0, 3, to)

        def spread_deep():
            for h in range(2):
                mine = result.at[job, h, rows(start3[h], SHARD)]
                for _, to in deep_peers():
                    remote(mine, mine, q0, 4, to)

        def step4():
            arrived(zrecv.at[pl.ds(0, g.deep - 1), job], q0, 3)
            for c, q, base, h in each_part:
                v = total[h, rows(base + start3[h], SHARD), :]
                for t, _ in deep_peers():
                    v = v + zrecv[t, q, h].astype(F32)
                if g.reps == 1:
                    result[q, h, rows(start3[h], SHARD), :] = v.astype(BF16)
                else:
                    total[h, rows(base + start3[h], SHARD), :] = v
                    zsend[deep_at, q, h] = v.astype(BF16)
            if g.reps == 1:
                spread_deep()
            else:
                for t, to in rep_peers():
                    remote(zsend.at[deep_at, job], rrecv.at[rep_at, job], q0, 7, to)

        def step4_more():
            arrived(rrecv.at[pl.ds(0, g.reps - 1), job], q0, 7)
            for c, q, base, h in each_part:
                v = total[h, rows(base + start3[h], SHARD), :]
                for t, _ in rep_peers():
                    v = v + rrecv[t, q, h].astype(F32)
                result[q, h, rows(start3[h], SHARD), :] = v.astype(BF16)
            spread_deep()

        def step5():
            arrived(zrecv.at[pl.ds(0, g.deep - 1), job], q0, 4)
            for h in range(2):
                mine = result.at[job, h, rows(start2[h], QUARTER)]
                remote(mine, mine, q0, 5, near[1 - h])

        def step6():
            arrived(yrecv.at[job], q0, 5)
            for h in range(2):
                mine = result.at[job, h, rows(start1[h], HALF)]
                remote(mine, mine, q0, 6, near[h])

        def step7():
            arrived(xrecv.at[job], q0, 6)
            kout = (kout1, kout2)[j]
            for c, q, base, h in each_part:
                pltpu.make_async_copy(result.at[q, h], kout.at[h, pl.ds(base, R), :], sem_res.at[q, h]).start()

        def done():
            for c, q, base, h in each_part:
                pltpu.make_async_copy(result.at[q, h], result.at[q, h], sem_res.at[q, h]).wait()
            left(xsend.at[job], q0, 1)
            left(ysend.at[job], q0, 2)
            left(zsend.at[pl.ds(0, g.deep - 1), job], q0, 3)
            left(zsend.at[pl.ds(0, g.deep - 1), job], q0, 4)
            left(ysend.at[job], q0, 5)
            left(xsend.at[job], q0, 6)
            if g.reps > 1:
                left(rrecv.at[pl.ds(0, g.reps - 1), job], q0, 7)

        middle = [step4] if g.reps == 1 else [step4, step4_more]
        return give, [step1, step2, step3] + middle + [step5, step6, step7], done

    clock, link = [0.0], [0.0]
    open_jobs, finals = [], []
    LATENCY = g.latency

    def begin(k, j, first_part, number):
        give, steps, done = job_steps(k, j, first_part, number)
        pl.when(sec != k)(give)
        use, wait = LATENCY[0]
        open_jobs.append([clock[0] + number * use + wait, k, steps, 0, number])
        finals.append((k, done))

    def advance(spent, go=True):
        clock[0] += spent
        if not go:
            return
        ready = sorted((job for job in open_jobs if job[0] <= clock[0]), key=lambda job: job[0])
        for k in range(2):

            @pl.when(sec == k)
            def _():
                for job in ready:
                    if job[1] == k:
                        run_step(job)

    def run_step(job):
        _, k, steps, at, number = job
        steps[at]()
        at += 1
        if at == len(steps):
            open_jobs.remove(job)
            return
        use, wait = LATENCY[at]
        link[0] = max(link[0], clock[0]) + number * use
        job[0], job[3] = link[0] + wait, at

    def drain(extra):
        at = 0
        while open_jobs:
            at += 1
            if at % 4 == 0 and extra:
                extra.pop(0)()
            job = min(open_jobs, key=lambda job: job[0])
            clock[0] = max(clock[0], job[0])
            pl.when(sec == job[1])(functools.partial(run_step, job))
        for rest in extra:
            rest()

    everyone = range(micro)
    cots = [load_in(cot, m, slot, sem_cot) for m, slot in enumerate((1, 0, 1))]
    load_field(0, 0, load_in(boards, 2, 0, sem_in))
    load_field(1, 1, cots[0])
    load_field(2, 0, cots[1])

    @pl.when(sec == 0)
    def _():
        own_w[0].wait()

    @pl.when(sec != 0)
    def _():
        pltpu.make_async_copy(w1.at[other], w1.at[other], sem_wr.at[0]).wait()

    each(first_conv)
    several = cinbox.at[pl.ds(0, n - 1)]
    pltpu.make_async_copy(several, several, sem_c.at[1]).wait()
    pltpu.make_async_copy(several, several, sem_c.at[0]).wait()
    totals[...] = jnp.sum(cinbox[...], axis=0)
    for c in own_w[1:]:
        c.wait()

    @pl.when(sec != 0)
    def _():
        own_w[0].wait()

    for ref, q in ((w2.at[other], 1), (gb.at[other, 0], 2), (gb.at[other, 1], 3)):
        pltpu.make_async_copy(ref, ref, sem_wr.at[q]).wait()
    cots[0].wait()
    spread(1, dp_.at[0])
    cots[2].start()
    each(second_conv(1, 0))

    @pl.when(sec == 0)
    def _():
        pltpu.make_async_copy(w1.at[other], w1.at[other], sem_wr.at[0]).wait()

    for c in send_w:
        c.wait_send()
    cots[1].wait()
    spread(0, dp_.at[1])
    for m in everyone:
        third_conv(m)
    cots[2].wait()
    spread(1, dp_.at[2])
    each(second_conv(3, 1))
    for m in everyone:
        turn(m)
        wait_out(m)
        gather(m, temp)
        emit(0, 1, m)

    chain = [(5, m) for m in everyone] + [(6, m) for m in everyone]

    def prepare(at):
        if at == 2 * micro:
            return second_prep(7, 0, 0, us.at[1, 0])
        phase, m = chain[at]
        return (second_prep if phase == 5 else first_prep)(phase, 1, m, ds.at[at % 2])

    prepare(0)()
    for at, (phase, m) in enumerate(chain):
        grad = ds.at[at % 2]
        (second_grad if phase == 5 else first_grad)(phase, 1, m, grad)
        following = prepare(at + 1)
        if phase == 5:
            kernel_grad(acc.at[1, 1], [(us.at[1, m], grad)], add=m > 0)
        else:
            kernel_grad(acc.at[1, 0], [(xs.at[1, m], grad)], add=m > 0)
        following()
        if phase == 6:
            advance(3.3, m != 1)
        if m == micro - 1:
            for c in range(g.parts):
                begin(1, 6 - phase, c, 1)

    for m in everyone:
        second_grad(7, 0, m, us.at[1, m])
        if m + 1 < micro:
            second_prep(7, 0, m + 1, us.at[1, m + 1])()
        advance(1.7, m != 1)
    taps = 9 // g.parts
    for c in range(g.parts):
        kernel_grad(acc.at[0, 1], [(us.at[0, m], us.at[1, m]) for m in everyone], range(c * taps, (c + 1) * taps))
        first_prep(8, 0, c, xs.at[1, c])()
        begin(0, 1, c, 1)
        advance(1.8)
    for c in range(g.parts):
        kernel_grad(acc.at[0, 0], [(xs.at[0, m], xs.at[1, m]) for m in everyone], range(c * taps, (c + 1) * taps))
        begin(0, 0, c, 1)
        advance(1.75)
    for m in everyone:
        wait_out(m)
        first_grad(8, 0, m, xs.at[1, m])
        gather(m, temp)
        emit(1, 0, m)
        advance(1.9)

    def late(m):
        wait_out(m + micro)
        gather(m + micro, h1.at[1, m])
        emit(1, 1, m, m + micro)


    swap = pltpu.make_async_remote_copy(gacc.at[other], grecv, sem_g.at[0], sem_g.at[1], device_id=partner, device_id_type=MESH)
    swap.start()
    drain([functools.partial(late, m) for m in everyone])
    swap.wait()
    gout[0] = gacc[sec, 0] + grecv[0]
    bout[0] = gacc[sec, 1] + grecv[1]
    for at in range(2):
        wait_out(at)
    for which, out in enumerate((hidden, igrads)):
        for k in range(2):
            for m in range(micro):
                came = out.at[lax.rem(sec + k, 2), other * micro + m]
                pltpu.make_async_copy(came, came, sem_outr.at[which, k, m]).wait()
    for c in range(g.parts):
        left(psend.at[c], c, 0)
    for k, done in finals:
        pl.when(sec == k)(done)


def local(n, boards, cotangent, counts, kernel_one, kernel_two, gains, biases):
    g = Plan()
    micro, slots, board, _, C = boards.shape
    g.n, g.half, g.slots, g.board, g.channels = n, micro // 2, slots, board, C
    half = g.half
    BT = board * TILE
    haloed = (AI + 2, (board + 2) * TILE, C)
    dense = (AI, BT, C)
    flat_kernel = (1, 9, C, C)
    g.parts = 3
    g.rows = 9 * C // g.parts
    g.deep = 4 if n % 16 == 0 else 1
    g.reps = n // (4 * g.deep)
    jobs = 2 * g.parts
    R = g.rows
    shard = R // 4 // g.deep
    g.latency = [(0.52, 0.54), (0.66, 1.56), (0.33, 1.56), (0.66, 1.8), (0.66, 1.8), (0.33, 1.56), (0.66, 1.56), (0.0, 0.0), (0.0, 0.0)]
    dma = pltpu.SemaphoreType.DMA
    scratch = [
        pltpu.VMEM((2, slots, board, board, C), BF16),
        pltpu.VMEM((2, slots, board, board, C), BF16),
        pltpu.VMEM((C // 128, AI, BT, 128), F32),
        pltpu.VMEM((2, half) + haloed, BF16),
        pltpu.VMEM((2, half) + haloed, BF16),
        pltpu.VMEM((2,) + haloed, BF16),
        pltpu.VMEM((2, half, C // 128, AI, BT, 128), F32),
        pltpu.VMEM((2, half) + dense, F32),
        pltpu.VMEM((half, C // 128, AI, BT, 128), F32),
        pltpu.VMEM((2, 9, C, C), BF16),
        pltpu.VMEM((2, 9, C, C), BF16),
        pltpu.VMEM((2, 2, 2, C), F32),
        pltpu.VMEM((2, 2, half, 8, C), F32),
        pltpu.VMEM((half, 2, TILE, C), F32),
        pltpu.VMEM((2, 2, 2, 9 * C, 128), F32),
        pltpu.VMEM((2, half, 4, 128), F32),
        pltpu.VMEM((2, half, n, 4, 128), F32),
        pltpu.VMEM((4, 128), F32),
        pltpu.VMEM((n, 4, 128), F32),
        pltpu.VMEM((4, 128), F32),
        pltpu.VMEM((2, 2, 2, C), F32),
        pltpu.VMEM((2, 2, C), F32),
        pltpu.SMEM((1, micro), jnp.int32),
        pltpu.VMEM((g.parts, 2, R, 128), BF16),
        pltpu.VMEM((g.parts, 2, R, 128), BF16),
        pltpu.VMEM((jobs, 2, R // 2, 128), BF16),
        pltpu.VMEM((jobs, 2, R // 2, 128), BF16),
        pltpu.VMEM((jobs, 2, R // 4, 128), BF16),
        pltpu.VMEM((jobs, 2, R // 4, 128), BF16),
        pltpu.VMEM((g.deep, jobs, 2, shard, 128), BF16),
        pltpu.VMEM((g.deep, jobs, 2, shard, 128), BF16),
        pltpu.VMEM((g.reps, jobs, 2, shard, 128) if g.reps > 1 else (1, 16, 128), BF16),
        pltpu.VMEM((jobs, 2, R, 128), BF16),
        dma((half,)), dma((half,)), dma((5,)), dma((4,)), dma((4,)),
        dma((2,)), dma((2,)), dma((2, 2, half)), dma((2, half)), dma((2, half)), dma((2,)), dma((2,)), dma((jobs, 9)), dma((jobs, 9)), dma((jobs, 2)),
        pltpu.SemaphoreType.REGULAR((g.parts,)),
    ]
    anywhere = pl.BlockSpec(memory_space=pl.ANY)
    vmem = pl.BlockSpec(memory_space=pltpu.VMEM)
    field = jax.ShapeDtypeStruct((1,) + boards.shape, BF16)
    fields = jax.ShapeDtypeStruct((2,) + boards.shape, BF16)
    grad = jax.ShapeDtypeStruct((2, 9 * C, 128), BF16)
    pair = jax.ShapeDtypeStruct(gains.shape, F32)
    hidden, igrads, k1, k2, gg, bg = pl.pallas_call(
        functools.partial(kernel, g),
        out_shape=(fields, fields, grad, grad, pair, pair),
        in_specs=[anywhere] * 7,
        out_specs=(anywhere, anywhere, anywhere, anywhere, vmem, vmem),
        scratch_shapes=scratch,
        compiler_params=pltpu.CompilerParams(collective_id=0, has_side_effects=True, vmem_limit_bytes=(63 * 16 + 14) * 2**16),
    )(
        boards, cotangent, counts.T, kernel_one.reshape(flat_kernel), kernel_two.reshape(flat_kernel), gains, biases
    )

    grad = jax.ShapeDtypeStruct(flat_kernel, F32)
    hidden, igrads, k1, k2, gg, bg = pl.pallas_call(
        finish,
        out_shape=(field, field, grad, grad, pair, pair),
        in_specs=[anywhere] * 6,
        out_specs=(anywhere,) * 6,
        scratch_shapes=[
            pltpu.VMEM((2,) + boards.shape, BF16),
            pltpu.VMEM((2, 2, 9 * C, 128), BF16),
            pltpu.VMEM((2, 9, C, C), F32),
            pltpu.VMEM((2,) + gains.shape, F32),
            dma((2, micro)), dma((2, micro)), dma((2,)), dma((2, 9)), dma((2,)), dma((2,)),
        ],
        compiler_params=pltpu.CompilerParams(vmem_limit_bytes=(63 * 16 + 14) * 2**16),
    )(hidden, igrads, k1, k2, gg, bg)
    return hidden, igrads, k1.reshape(kernel_one.shape), k2.reshape(kernel_two.shape), gg, bg


def finish(hidden, igrads, k1, k2, gg, bg, hidden_out, igrads_out, k1_out, k2_out, gg_out, bg_out, fields, narrow, wide, small, *sems):
    sem_in, sem_out, sem_k, sem_kout, sem_s, sem_sout = sems
    C = wide.shape[2]
    copies = pltpu.make_async_copy
    loads, stores = [], []
    for q, (src, dst) in enumerate(((gg, gg_out), (bg, bg_out))):
        loads.append(copies(src, small.at[q], sem_s.at[q]))
        stores.append(copies(small.at[q], dst, sem_sout.at[q]))
    kernels = [copies(src, narrow.at[q], sem_k.at[q]) for q, src in enumerate((k1, k2))]
    for q, (src, dst) in enumerate(((hidden, hidden_out), (igrads, igrads_out))):
        for m in range(src.shape[1]):
            loads.append(copies(src.at[0, m], fields.at[q, m], sem_in.at[q, m]))
            stores.append(copies(fields.at[q, m], dst.at[0, m], sem_out.at[q, m]))
    for c in kernels + loads:
        c.start()
    wides = []
    for q, dst in enumerate((k1_out, k2_out)):
        kernels[q].wait()
        for t in range(9):
            for h in range(2):
                wide[q, t, :, pl.ds(128 * h, 128)] = narrow[q, h, pl.ds(t * C, C), :].astype(F32)
            c = copies(wide.at[q, t], dst.at[0, t], sem_kout.at[q, t])
            c.start()
            wides.append(c)
    for load, store in zip(loads, stores):
        load.wait()
        store.start()
    for c in stores + wides:
        c.wait()


def solution(mesh):
    return jax.shard_map(
        functools.partial(local, mesh.shape["dp"]),
        mesh=mesh,
        in_specs=(
            P(None, "dp", None, None, None),
            P(None, "dp", None, None, None),
            P(None, "dp"),
            P("section", None, None, None, None),
            P("section", None, None, None, None),
            P("section", None, None),
            P("section", None, None),
        ),
        out_specs=(
            P("section", None, "dp", None, None, None),
            P("section", None, "dp", None, None, None),
            P("section", None, None, None, None),
            P("section", None, None, None, None),
            P("section", None, None),
            P("section", None, None),
        ),
        check_vma=False,
    )
```

```python
import functools

import jax
import jax.numpy as jnp
from jax import lax
from jax.experimental import pallas as pl
from jax.experimental.pallas import tpu as pltpu
from jax.sharding import PartitionSpec as P

MESH = pl.DeviceIdType.MESH
F32, BF16 = jnp.float32, jnp.bfloat16

STRIPS, AI, TILE = 5, 4, 16


class Plan:
    pass


def kernel(g, *refs):
    (
        boards, cot, counts, kone, ktwo, gains, biases,
        hidden, igrads, kout1, kout2, gout, bout,
        stage, ostage, temp, xs, us, ds, h1, h2, dp_, w1, w2, gb, coef, masks, acc, msg, inbox, cmsg, cinbox, totals, gacc, grecv, filled_here,
        psend, precv, xsend, xrecv, ysend, yrecv, zsend, zrecv, rrecv, result,
        sem_in, sem_cot, sem_w, sem_wr, sem_ws, sem_out, sem_outs, sem_outr, sem_msg, sem_inbox, sem_c, sem_g, sem_js, sem_jr, sem_res, sem_free,
    ) = refs
    dy_ = h2.at[1]
    n, micro, slots, board, C = g.n, g.half, g.slots, g.board, g.channels
    BT = board * TILE
    me = lax.axis_index("dp")
    sec = lax.axis_index("section")
    other = 1 - sec
    partner = {"section": other}
    first = sec * micro

    def load_in(src, m, slot, sem):
        return pltpu.make_async_copy(src.at[first + m], stage.at[slot], sem.at[m])

    barrier = pltpu.get_barrier_semaphore()

    def greet(i, _):
        pl.semaphore_signal(barrier, inc=1, device_id={"dp": lax.rem(me + i, n)}, device_id_type=MESH)
        return 0

    pl.semaphore_signal(barrier, inc=1, device_id=partner, device_id_type=MESH)
    lax.fori_loop(1, n, greet, 0, unroll=n <= 16)
    count_in = pltpu.make_async_copy(counts, filled_here, sem_w.at[4])
    count_in.start()
    for m in range(2):
        load_in(boards, m, m, sem_in).start()
    own_w = [
        pltpu.make_async_copy(kone.at[0], w1.at[sec], sem_w.at[0]),
        pltpu.make_async_copy(ktwo.at[0], w2.at[sec], sem_w.at[1]),
        pltpu.make_async_copy(gains.at[0], gb.at[sec, 0], sem_w.at[2]),
        pltpu.make_async_copy(biases.at[0], gb.at[sec, 1], sem_w.at[3]),
    ]
    for c in own_w:
        c.start()
    pl.semaphore_wait(barrier, n)
    send_w = [
        pltpu.make_async_remote_copy(kone.at[0], w1.at[sec], sem_ws.at[0], sem_wr.at[0], device_id=partner, device_id_type=MESH),
        pltpu.make_async_remote_copy(gains.at[0], gb.at[sec, 0], sem_ws.at[2], sem_wr.at[2], device_id=partner, device_id_type=MESH),
        pltpu.make_async_remote_copy(biases.at[0], gb.at[sec, 1], sem_ws.at[3], sem_wr.at[3], device_id=partner, device_id_type=MESH),
        pltpu.make_async_remote_copy(ktwo.at[0], w2.at[sec], sem_ws.at[1], sem_wr.at[1], device_id=partner, device_id_type=MESH),
    ]
    for c in send_w:
        c.start()

    def peers(ship):
        if n <= 16 and n & (n - 1) == 0:
            bits = [lax.rem(me // 2**b, 2) for b in range(n.bit_length() - 1)]
            for i in range(n - 1, 0, -1):
                ship(sum((1 - bit if i >> b & 1 else bit) * 2**b for b, bit in enumerate(bits)))
        else:

            def one(i, _):
                ship(lax.rem(me + i, n))
                return 0

            lax.fori_loop(1, n, one, 0)

    count_in.wait()
    entry = lax.broadcasted_iota(jnp.int32, (TILE, C), 0)
    slot = lax.rem(entry, slots)
    cmsg[...] = jnp.zeros_like(cmsg)
    for m in range(micro):
        filled = jnp.logical_and(slot < filled_here[0, first + m], entry < STRIPS * slots)
        masks[m, 0] = filled.astype(F32)
        masks[m, 1] = jnp.logical_and(filled, entry < (STRIPS - 1) * slots).astype(F32)

        cmsg[pl.ds(m, 1), :] = jnp.full((1, 128), filled_here[0, first + m].astype(F32) * float(board * board), F32)
    cinbox[me] = cmsg[...]
    peers(
        lambda to: pltpu.make_async_remote_copy(
            cmsg, cinbox.at[me], sem_c.at[0], sem_c.at[1], device_id={"dp": to}, device_id_type=MESH
        ).start()
    )
    edge = jnp.zeros((6, TILE, C), BF16)

    def clear(m, _):
        for ref in (xs.at[0], xs.at[1], us.at[0], us.at[1]):
            ref[m, :, pl.ds(0, TILE), :] = edge
            ref[m, :, pl.ds((board + 1) * TILE, TILE), :] = edge
        return 0

    lax.fori_loop(0, micro, clear, 0)
    for q in range(2):
        ds[q, :, pl.ds(0, TILE), :] = edge
        ds[q, :, pl.ds((board + 1) * TILE, TILE), :] = edge
    temp[...] = jnp.zeros_like(temp)
    dp_[...] = jnp.zeros_like(dp_)
    gacc[...] = jnp.zeros_like(gacc)

    def mask_of(m, ai):
        return masks[m, 1 if ai == AI - 1 else 0][None]

    def tiles(v):
        return v.reshape(board, TILE, C)

    def flat(v):
        return v.reshape(BT, C)

    def put(ref, ai, value):
        ref[ai + 1, pl.ds(TILE, BT), :] = flat(value).astype(BF16)
        if ai == AI - 1:
            ref[0, pl.ds(TILE, BT), :] = flat(pltpu.roll(value, slots, 1)).astype(BF16)
        if ai == 0:
            ref[AI + 1, pl.ds(TILE, BT), :] = flat(pltpu.roll(value, TILE - slots, 1)).astype(BF16)

    def window(ref, ai, i, j):
        return ref[ai + i, pl.ds(j * TILE, BT), :]

    def inner(ref, ai):
        return window(ref, ai, 1, 1)

    def conv(ref, ai, weights):
        lhs = jnp.concatenate([window(ref, ai, i, j) for i in range(3) for j in range(3)], axis=1)
        return jnp.dot(lhs, weights[...], preferred_element_type=F32)

    def conv_back(ref, ai, weights):
        out = None
        for i in range(3):
            for j in range(3):
                part = lax.dot_general(
                    window(ref, ai, i, j), weights[pl.ds((8 - 3 * i - j) * C, C), :], (((1,), (1,)), ((), ())), preferred_element_type=F32
                )
                out = part if out is None else out + part
        return out

    def kernel_grad(total, pairs, taps=range(9), add=False):
        lhs = jnp.concatenate([inner(ref, ai) for ref, _ in pairs for ai in range(AI)], axis=0)
        for t in taps:
            i, j = t // 3, t % 3
            rhs = jnp.concatenate([window(grad, ai, 2 - i, 2 - j) for _, grad in pairs for ai in range(AI)], axis=0)
            d = lax.dot_general(lhs, rhs, (((0,), (0,)), ((), ())), preferred_element_type=F32)
            for h in range(2):
                at, part = (h, pl.ds(t * C, C)), d[:, 128 * h : 128 * (h + 1)]
                total[at] = total[at] + part if add else part

    def fold(v):
        return jnp.sum(v.reshape(BT // 8, 8, C), axis=0)

    def send_stats(phase, m, one, two):
        par = phase % 2
        one = jnp.sum(one, axis=0, keepdims=True)
        two = jnp.sum(two, axis=0, keepdims=True)
        for r, v in enumerate((one[:, :128], one[:, 128:], two[:, :128], two[:, 128:])):
            msg[par, m, pl.ds(r, 1), :] = v
        inbox[par, m, me] = msg[par, m]
        peers(
            lambda to: pltpu.make_async_remote_copy(
                msg.at[par, m], inbox.at[par, m, me], sem_msg.at[par, m], sem_inbox.at[par, m],
                device_id={"dp": to}, device_id_type=MESH,
            ).start()
        )

    def get_stats(phase, m):
        par = phase % 2
        several = inbox.at[par, m, pl.ds(0, n - 1)]
        pltpu.make_async_copy(several, several, sem_inbox.at[par, m]).wait()
        pltpu.make_async_copy(several, several, sem_msg.at[par, m]).wait()
        if n <= 16:
            total = inbox[par, m, 0]
            for d in range(1, n):
                total = total + inbox[par, m, d]
        else:
            total = jnp.sum(inbox[par, m], axis=0)
        one = jnp.concatenate([total[0:1], total[1:2]], axis=1)
        two = jnp.concatenate([total[2:3], total[3:4]], axis=1)
        return one, two

    def norm_coefs(phase, m, k, j):
        one, two = get_stats(phase, m)
        count = jnp.concatenate([totals[pl.ds(m, 1), :]] * (C // 128), axis=1)
        mean = one / count
        var = two / count - mean * mean
        r = lax.rsqrt(var + 1e-5)
        scale = r * gb[k, 0, pl.ds(j, 1), :]
        offset = gb[k, 1, pl.ds(j, 1), :] - mean * scale
        for q, v in enumerate((0.5 * scale, 0.5 * offset, r, mean, count, scale)):
            coef[k, j, m, pl.ds(q, 1), :] = v
        return 0.5 * scale, 0.5 * offset

    def kept(m, k, j):
        return coef[k, j, m, pl.ds(0, 1), :], coef[k, j, m, pl.ds(1, 1), :]

    def back_coefs(phase, m, k, j):
        sdy, sdh = get_stats(phase, m)
        r, mean = coef[k, j, m, pl.ds(2, 1), :], coef[k, j, m, pl.ds(3, 1), :]
        count, alpha = coef[k, j, m, pl.ds(4, 1), :], coef[k, j, m, pl.ds(5, 1), :]
        sdx = r * (sdh - mean * sdy)
        gacc[k, 0, pl.ds(j, 1), :] += sdx
        gacc[k, 1, pl.ds(j, 1), :] += sdy
        gamma = -alpha * r * sdx / count
        beta = -alpha * sdy / count - gamma * mean
        return alpha, gamma, beta

    def silu2(z):
        return z + z * jnp.tanh(z)

    def slope2(z):
        t = jnp.tanh(z)
        return (0.5 + 0.5 * t) * (1.0 + z * (1.0 - t))

    def places():
        return [(p, a) for p in range(slots) for a in range(board)]

    FIELD = C // 128 * AI * BT

    def temp_field():
        return temp, 0

    def dp_field(m):
        return dp_, m * FIELD

    def h1_field(k, m):
        return h1, (k * micro + m) * FIELD

    def split_rows(field, c, ai):
        return pl.ds(pl.multiple_of(field[1] + (c * AI + ai) * BT, TILE), BT)

    def strided(field, c, p, a):
        return pl.ds(field[1] + (c * AI + a % AI) * BT + a // AI * slots + p, board, TILE)

    def spread(slot, to):
        for p, a in places():
            for c in range(C // 128):
                to[0][strided(to, c, p, a), :] = stage[slot, p, a, :, pl.ds(128 * c, 128)].astype(F32)

    def gather(m, source):
        for p, a in places():
            for c in range(C // 128):
                ostage[lax.rem(m, 2), p, a, :, pl.ds(128 * c, 128)] = source[0][strided(source, c, p, a), :].astype(BF16)

    def read_split(field, ai):
        return jnp.concatenate([field[0][split_rows(field, c, ai), :] for c in range(C // 128)], axis=1)

    def write_split(field, ai, v):
        for c in range(C // 128):
            field[0][split_rows(field, c, ai), :] = v[:, 128 * c : 128 * (c + 1)]

    def wait_out(at):
        o = lax.rem(at, 2)
        for sems in (sem_out, sem_outs):
            pltpu.make_async_copy(ostage.at[o], ostage.at[o], sems.at[o]).wait()

    def emit(which, k, m, at=None):
        out = (hidden, igrads)[which]
        o = lax.rem(m if at is None else at, 2)
        away = lax.rem(sec + k, 2)
        pltpu.make_async_copy(ostage.at[o], out.at[away, first + m], sem_out.at[o]).start()
        pltpu.make_async_remote_copy(
            ostage.at[o], out.at[1 - away, first + m], sem_outs.at[o], sem_outr.at[which, k, m], device_id=partner, device_id_type=MESH
        ).start()

    def each(body):
        def step(m, _):
            body(m)
            return 0

        lax.fori_loop(0, micro, step, 0)

    def run_conv(phase, m, ref, weights, write):
        one = two = jnp.zeros((8, C), F32)
        for ai in range(AI):
            h = conv(ref, ai, weights)
            write(ai, h)
            if ai == AI - 1:
                h = flat(tiles(h) * mask_of(m, ai))
            one = one + fold(h)
            two = two + fold(h * h)
        send_stats(phase, m, one, two)

    ORDER = (AI - 1,) + tuple(range(AI - 1))

    def load_field(m, slot, following):
        load_in(boards, m, slot, sem_in).wait()
        spread(slot, temp_field())
        following.start()
        for ai in ORDER:
            put(xs.at[0, m], ai, tiles(read_split(temp_field(), ai)) * mask_of(m, ai))

    def first_conv(m):
        run_conv(0, m, xs.at[0, m], w1.at[0], functools.partial(write_split, h1_field(0, m)))

    def second_conv(phase, k):
        def body(m):
            a, b = norm_coefs(phase - 1, m, k, 0)
            for ai in ORDER:
                put(us.at[k, m], ai, tiles(silu2(read_split(h1_field(k, m), ai) * a + b)) * mask_of(m, ai))

            def write(ai, h):
                h2[k, m, ai] = h

            run_conv(phase, m, us.at[k, m], w2.at[k], write)

        return body

    def third_conv(m):
        if m >= 2:
            wait_out(m)
        a, b = norm_coefs(1, m, 0, 1)
        for ai in ORDER:
            z = h2[0, m, ai] * a + b + 0.5 * inner(xs.at[0, m], ai).astype(F32)
            x = tiles(silu2(z)) * mask_of(m, ai)
            put(xs.at[1, m], ai, x)
            write_split(temp_field(), ai, flat(x))
        run_conv(2, m, xs.at[1, m], w1.at[1], functools.partial(write_split, h1_field(1, m)))
        gather(m, temp_field())
        emit(0, 0, m)

    def turn(m):
        a, b = norm_coefs(3, m, 1, 1)
        one = two = jnp.zeros((8, C), F32)
        for ai in range(AI):
            h = h2[1, m, ai]
            z = h * a + b + 0.5 * inner(xs.at[1, m], ai).astype(F32)
            t = jnp.tanh(z)
            mask = mask_of(m, ai)
            write_split(temp_field(), ai, flat(tiles(z + z * t) * mask))
            slope = (0.5 + 0.5 * t) * (1.0 + z * (1.0 - t))
            dy = flat(tiles(read_split(dp_field(m), ai) * slope) * mask)
            write_split(dp_field(m), ai, dy)
            one = one + fold(dy)
            two = two + fold(dy * h)
        send_stats(4, m, one, two)

    def second_prep(phase, k, m, grad):
        alpha, gamma, beta = back_coefs(phase - 1, m, k, 1)

        def go():
            for ai in ORDER:
                put(grad, ai, tiles(alpha * read_split(dp_field(m), ai) + gamma * h2[k, m, ai] + beta) * mask_of(m, ai))

        return go

    def second_grad(phase, k, m, grad):
        a, b = kept(m, k, 0)
        one = two = jnp.zeros((8, C), F32)
        for ai in range(AI):
            du = conv_back(grad, ai, w2.at[k])
            h = read_split(h1_field(k, m), ai)
            dy = du * slope2(h * a + b)
            if ai == AI - 1:
                dy = flat(tiles(dy) * mask_of(m, ai))
            dy_[m, ai] = dy
            one = one + fold(dy)
            two = two + fold(dy * h)
        send_stats(phase, m, one, two)

    def first_prep(phase, k, m, grad):
        alpha, gamma, beta = back_coefs(phase - 1, m, k, 0)

        def go():
            for ai in ORDER:
                put(grad, ai, tiles(alpha * dy_[m, ai] + gamma * read_split(h1_field(k, m), ai) + beta) * mask_of(m, ai))

        return go

    def first_grad(phase, k, m, grad):
        if k == 1:
            a, b = kept(m, 0, 1)
            one = two = jnp.zeros((8, C), F32)
        for ai in range(AI):
            dx = (conv_back(grad, ai, w1.at[k]) + read_split(dp_field(m), ai)).astype(BF16).astype(F32)
            write_split(h1_field(1, m) if k == 1 else temp_field(), ai, dx)
            if k == 1:
                h = h2[0, m, ai]
                z = h * a + b + 0.5 * inner(xs.at[0, m], ai).astype(F32)
                dy = dx * slope2(z)
                if ai == AI - 1:
                    dy = flat(tiles(dy) * mask_of(m, ai))
                write_split(dp_field(m), ai, dy)
                one = one + fold(dy)
                two = two + fold(dy * h)
        if k == 1:
            send_stats(phase, m, one, two)

    R = g.rows
    HALF, QUARTER, SHARD = R // 2, R // 4, R // 4 // g.deep
    bit0, bit1 = lax.rem(me, 2), lax.rem(me // 2, 2)
    deep_at = lax.rem(me // 4, g.deep)
    rep_at = me // (4 * g.deep)
    near = ({"dp": me + 1 - 2 * bit0}, {"dp": me + 2 - 4 * bit1})
    order = ((bit0, bit1), (bit1, bit0))

    def rows(start, size):
        return pl.ds(pl.multiple_of(start, 16), size)

    def remote(src, dst, job, step, to):
        pltpu.make_async_remote_copy(src, dst, sem_js.at[job, step], sem_jr.at[job, step], device_id=to, device_id_type=MESH).start()

    def arrived(ref, job, step):
        pltpu.make_async_copy(ref, ref, sem_jr.at[job, step]).wait()

    def left(ref, job, step):
        pltpu.make_async_copy(ref, ref, sem_js.at[job, step]).wait()

    def deep_peers():
        for i in range(1, g.deep):
            t = lax.rem(deep_at + i, g.deep)
            yield t, {"dp": me + (t - deep_at) * 4}

    def rep_peers():
        for i in range(1, g.reps):
            t = lax.rem(rep_at + i, g.reps)
            yield t, {"dp": me + (t - rep_at) * 4 * g.deep}

    def job_steps(k, j, first_part, number):
        parts = range(first_part, first_part + number)
        span = pl.ds(first_part, number)
        q0 = j * g.parts + first_part
        job = pl.ds(q0, number)
        total = acc.at[k, j]
        start1 = [order[h][0] * HALF for h in range(2)]
        start2 = [start1[h] + order[h][1] * QUARTER for h in range(2)]
        start3 = [start2[h] + deep_at * SHARD for h in range(2)]
        last = (k, j) == (0, 0)

        def sending(c):
            return w2.at[0, pl.ds(c * R, R)] if last else psend.at[c]

        def coming(c):
            return w2.at[1, pl.ds(c * R, R)] if last else precv.at[c]

        def came_in(c, h, start, size):
            if last:
                return w2[1, rows(c * R + start, size), pl.ds(128 * h, 128)].astype(F32)
            return precv[c, h, rows(start, size), :].astype(F32)

        each_part = [(c, j * g.parts + c, c * R, h) for c in parts for h in range(2)]

        def give():
            if (k, j) == (1, 0):
                for c in parts:
                    left(psend.at[c], c, 8)
                    pl.semaphore_wait(sem_free.at[c], 1)
            for c, q, base, h in each_part:
                v = total[h, pl.ds(base, R), :].astype(BF16)
                if last:
                    w2[0, pl.ds(c * R, R), pl.ds(128 * h, 128)] = v
                else:
                    psend[c, h] = v
            for c in parts:
                pltpu.make_async_remote_copy(
                    sending(c), coming(c), sem_js.at[c, 8 * j], sem_jr.at[j * g.parts + c, 0], device_id=partner, device_id_type=MESH
                ).start()

        def step1():
            for c, q, base, h in each_part:
                if h == 0:
                    arrived(coming(c), q, 0)
                away = (1 - order[h][0]) * HALF
                xsend[q, h] = (total[h, rows(base + away, HALF), :] + came_in(c, h, away, HALF)).astype(BF16)
            for h in range(2):
                remote(xsend.at[job, h], xrecv.at[job, h], q0, 1, near[h])
            for c, q, base, h in each_part:
                total[h, rows(base + start1[h], HALF), :] += came_in(c, h, start1[h], HALF)
            if (k, j) == (1, 1):
                for c in parts:
                    pl.semaphore_signal(sem_free.at[c], inc=1, device_id=partner, device_id_type=MESH)

        def step2():
            arrived(xrecv.at[job], q0, 1)
            for c, q, base, h in each_part:
                away = (1 - order[h][1]) * QUARTER
                ysend[q, h] = (
                    total[h, rows(base + start1[h] + away, QUARTER), :] + xrecv[q, h, rows(away, QUARTER), :].astype(F32)
                ).astype(BF16)
            for h in range(2):
                remote(ysend.at[job, h], yrecv.at[job, h], q0, 2, near[1 - h])
            for c, q, base, h in each_part:
                keep = order[h][1] * QUARTER
                total[h, rows(base + start2[h], QUARTER), :] += xrecv[q, h, rows(keep, QUARTER), :].astype(F32)

        def step3():
            arrived(yrecv.at[job], q0, 2)
            for c, q, base, h in each_part:
                v = total[h, rows(base + start2[h], QUARTER), :] + yrecv[q, h].astype(F32)
                total[h, rows(base + start2[h], QUARTER), :] = v
                v = v.astype(BF16)
                for t in range(g.deep):
                    zsend[t, q, h] = v[t * SHARD : (t + 1) * SHARD]
            for t, to in deep_peers():
                remote(zsend.at[t, job], zrecv.at[deep_at, job], q0, 3, to)

        def spread_deep():
            for h in range(2):
                mine = result.at[job, h, rows(start3[h], SHARD)]
                for _, to in deep_peers():
                    remote(mine, mine, q0, 4, to)

        def step4():
            arrived(zrecv.at[pl.ds(0, g.deep - 1), job], q0, 3)
            for c, q, base, h in each_part:
                v = total[h, rows(base + start3[h], SHARD), :]
                for t, _ in deep_peers():
                    v = v + zrecv[t, q, h].astype(F32)
                if g.reps == 1:
                    result[q, h, rows(start3[h], SHARD), :] = v.astype(BF16)
                else:
                    total[h, rows(base + start3[h], SHARD), :] = v
                    zsend[deep_at, q, h] = v.astype(BF16)
            if g.reps == 1:
                spread_deep()
            else:
                for t, to in rep_peers():
                    remote(zsend.at[deep_at, job], rrecv.at[rep_at, job], q0, 7, to)

        def step4_more():
            arrived(rrecv.at[pl.ds(0, g.reps - 1), job], q0, 7)
            for c, q, base, h in each_part:
                v = total[h, rows(base + start3[h], SHARD), :]
                for t, _ in rep_peers():
                    v = v + rrecv[t, q, h].astype(F32)
                result[q, h, rows(start3[h], SHARD), :] = v.astype(BF16)
            spread_deep()

        def step5():
            arrived(zrecv.at[pl.ds(0, g.deep - 1), job], q0, 4)
            for h in range(2):
                mine = result.at[job, h, rows(start2[h], QUARTER)]
                remote(mine, mine, q0, 5, near[1 - h])

        def step6():
            arrived(yrecv.at[job], q0, 5)
            for h in range(2):
                mine = result.at[job, h, rows(start1[h], HALF)]
                remote(mine, mine, q0, 6, near[h])

        def step7():
            arrived(xrecv.at[job], q0, 6)
            kout = (kout1, kout2)[j]
            for c, q, base, h in each_part:
                pltpu.make_async_copy(result.at[q, h], kout.at[h, pl.ds(base, R), :], sem_res.at[q, h]).start()

        def done():
            for c, q, base, h in each_part:
                pltpu.make_async_copy(result.at[q, h], result.at[q, h], sem_res.at[q, h]).wait()
            left(xsend.at[job], q0, 1)
            left(ysend.at[job], q0, 2)
            left(zsend.at[pl.ds(0, g.deep - 1), job], q0, 3)
            left(zsend.at[pl.ds(0, g.deep - 1), job], q0, 4)
            left(ysend.at[job], q0, 5)
            left(xsend.at[job], q0, 6)
            if g.reps > 1:
                left(rrecv.at[pl.ds(0, g.reps - 1), job], q0, 7)

        middle = [step4] if g.reps == 1 else [step4, step4_more]
        return give, [step1, step2, step3] + middle + [step5, step6, step7], done

    clock, link = [0.0], [0.0]
    open_jobs, finals = [], []
    LATENCY = g.latency

    def begin(k, j, first_part, number):
        give, steps, done = job_steps(k, j, first_part, number)
        pl.when(sec != k)(give)
        use, wait = LATENCY[0]
        open_jobs.append([clock[0] + number * use + wait, k, steps, 0, number])
        finals.append((k, done))

    def advance(spent, go=True):
        clock[0] += spent
        if not go:
            return
        ready = sorted((job for job in open_jobs if job[0] <= clock[0]), key=lambda job: job[0])
        for k in range(2):

            @pl.when(sec == k)
            def _():
                for job in ready:
                    if job[1] == k:
                        run_step(job)

    def run_step(job):
        _, k, steps, at, number = job
        steps[at]()
        at += 1
        if at == len(steps):
            open_jobs.remove(job)
            return
        use, wait = LATENCY[at]
        link[0] = max(link[0], clock[0]) + number * use
        job[0], job[3] = link[0] + wait, at

    def drain(extra):
        due = clock[0]
        while open_jobs:
            job = min(open_jobs, key=lambda job: job[0])
            clock[0] = max(clock[0], job[0])
            if extra and clock[0] >= due:
                extra.pop(0)()
                due = clock[0] + g.pause
            pl.when(sec == job[1])(functools.partial(run_step, job))
        for rest in extra:
            rest()

    everyone = range(micro)
    cots = [load_in(cot, m, slot, sem_cot) for m, slot in enumerate((1, 0, 1))]
    load_field(0, 0, load_in(boards, 2, 0, sem_in))
    load_field(1, 1, cots[0])
    load_field(2, 0, cots[1])

    @pl.when(sec == 0)
    def _():
        own_w[0].wait()

    @pl.when(sec != 0)
    def _():
        pltpu.make_async_copy(w1.at[other], w1.at[other], sem_wr.at[0]).wait()

    each(first_conv)
    several = cinbox.at[pl.ds(0, n - 1)]
    pltpu.make_async_copy(several, several, sem_c.at[1]).wait()
    pltpu.make_async_copy(several, several, sem_c.at[0]).wait()
    totals[...] = jnp.sum(cinbox[...], axis=0)
    for c in own_w[1:]:
        c.wait()

    @pl.when(sec != 0)
    def _():
        own_w[0].wait()

    for ref, q in ((w2.at[other], 1), (gb.at[other, 0], 2), (gb.at[other, 1], 3)):
        pltpu.make_async_copy(ref, ref, sem_wr.at[q]).wait()
    cots[0].wait()
    spread(1, dp_field(0))
    cots[2].start()
    each(second_conv(1, 0))

    @pl.when(sec == 0)
    def _():
        pltpu.make_async_copy(w1.at[other], w1.at[other], sem_wr.at[0]).wait()

    for c in send_w:
        c.wait_send()
    cots[1].wait()
    spread(0, dp_field(1))
    for m in everyone:
        third_conv(m)
    cots[2].wait()
    spread(1, dp_field(2))
    each(second_conv(3, 1))
    for m in everyone:
        turn(m)
        wait_out(m)
        gather(m, temp_field())
        emit(0, 1, m)

    chain = [(5, m) for m in everyone] + [(6, m) for m in everyone]

    def prepare(at):
        if at == 2 * micro:
            return second_prep(7, 0, 0, us.at[1, 0])
        phase, m = chain[at]
        return (second_prep if phase == 5 else first_prep)(phase, 1, m, ds.at[at % 2])

    prepare(0)()
    for at, (phase, m) in enumerate(chain):
        grad = ds.at[at % 2]
        (second_grad if phase == 5 else first_grad)(phase, 1, m, grad)
        following = prepare(at + 1)
        if phase == 5:
            kernel_grad(acc.at[1, 1], [(us.at[1, m], grad)], add=m > 0)
        else:
            kernel_grad(acc.at[1, 0], [(xs.at[1, m], grad)], add=m > 0)
        following()
        if phase == 6:
            advance(3.3, m != 1)
        if m == micro - 1:
            for c in range(g.parts):
                begin(1, 6 - phase, c, 1)

    for m in everyone:
        second_grad(7, 0, m, us.at[1, m])
        if m + 1 < micro:
            second_prep(7, 0, m + 1, us.at[1, m + 1])()
        advance(1.7, m != 1)
    taps = 9 // g.parts
    for c in range(g.parts):
        kernel_grad(acc.at[0, 1], [(us.at[0, m], us.at[1, m]) for m in everyone], range(c * taps, (c + 1) * taps))
        first_prep(8, 0, c, xs.at[1, c])()
        begin(0, 1, c, 1)
        advance(1.8)
    for c in range(g.parts):
        kernel_grad(acc.at[0, 0], [(xs.at[0, m], xs.at[1, m]) for m in everyone], range(c * taps, (c + 1) * taps))
        begin(0, 0, c, 1)
        advance(1.75)
    for m in everyone:
        wait_out(m)
        first_grad(8, 0, m, xs.at[1, m])
        gather(m, temp_field())
        emit(1, 0, m)
        advance(1.9)

    def late(m):
        wait_out(m + micro)
        gather(m + micro, h1_field(1, m))
        emit(1, 1, m, m + micro)


    swap = pltpu.make_async_remote_copy(gacc.at[other], grecv, sem_g.at[0], sem_g.at[1], device_id=partner, device_id_type=MESH)
    swap.start()
    drain([functools.partial(late, m) for m in everyone])
    swap.wait()
    gout[0] = gacc[sec, 0] + grecv[0]
    bout[0] = gacc[sec, 1] + grecv[1]
    for at in range(2):
        wait_out(at)
    for which, out in enumerate((hidden, igrads)):
        for k in range(2):
            for m in range(micro):
                came = out.at[lax.rem(sec + k, 2), other * micro + m]
                pltpu.make_async_copy(came, came, sem_outr.at[which, k, m]).wait()
    for c in range(g.parts):
        left(psend.at[c], c, 0)

        @pl.when(sec == 1)
        def _():
            left(psend.at[c], c, 8)

    for k, done in finals:
        pl.when(sec == k)(done)


def local(n, boards, cotangent, counts, kernel_one, kernel_two, gains, biases):
    g = Plan()
    micro, slots, board, _, C = boards.shape
    g.n, g.half, g.slots, g.board, g.channels = n, micro // 2, slots, board, C
    half = g.half
    BT = board * TILE
    haloed = (AI + 2, (board + 2) * TILE, C)
    dense = (AI, BT, C)
    split = C // 128 * AI * BT
    spare = 5 * TILE
    flat_kernel = (1, 9, C, C)
    tall_kernel = (1, 9 * C, C)
    g.parts = 3
    g.rows = 9 * C // g.parts
    g.deep = 4 if n % 16 == 0 else 1
    g.reps = n // (4 * g.deep)
    jobs = 2 * g.parts
    R = g.rows
    shard = R // 4 // g.deep
    g.pause = 1.0
    g.latency = [(0.52, 0.54), (0.66, 1.56), (0.33, 1.56), (0.66, 1.8), (0.66, 1.8), (0.33, 1.56), (0.66, 1.56), (0.0, 0.0), (0.0, 0.0)]
    dma = pltpu.SemaphoreType.DMA
    scratch = [
        pltpu.VMEM((2, slots, board, board, C), BF16),
        pltpu.VMEM((2, slots, board, board, C), BF16),
        pltpu.VMEM((split + spare, 128), F32),
        pltpu.VMEM((2, half) + haloed, BF16),
        pltpu.VMEM((2, half) + haloed, BF16),
        pltpu.VMEM((2,) + haloed, BF16),
        pltpu.VMEM((2 * half * split + spare, 128), F32),
        pltpu.VMEM((2, half) + dense, F32),
        pltpu.VMEM((half * split + spare, 128), F32),
        pltpu.VMEM((2, 9 * C, C), BF16),
        pltpu.VMEM((2, 9 * C, C), BF16),
        pltpu.VMEM((2, 2, 2, C), F32),
        pltpu.VMEM((2, 2, half, 8, C), F32),
        pltpu.VMEM((half, 2, TILE, C), F32),
        pltpu.VMEM((2, 2, 2, 9 * C, 128), F32),
        pltpu.VMEM((2, half, 4, 128), F32),
        pltpu.VMEM((2, half, n, 4, 128), F32),
        pltpu.VMEM((4, 128), F32),
        pltpu.VMEM((n, 4, 128), F32),
        pltpu.VMEM((4, 128), F32),
        pltpu.VMEM((2, 2, 2, C), F32),
        pltpu.VMEM((2, 2, C), F32),
        pltpu.SMEM((1, micro), jnp.int32),
        pltpu.VMEM((g.parts, 2, R, 128), BF16),
        pltpu.VMEM((g.parts, 2, R, 128), BF16),
        pltpu.VMEM((jobs, 2, R // 2, 128), BF16),
        pltpu.VMEM((jobs, 2, R // 2, 128), BF16),
        pltpu.VMEM((jobs, 2, R // 4, 128), BF16),
        pltpu.VMEM((jobs, 2, R // 4, 128), BF16),
        pltpu.VMEM((g.deep, jobs, 2, shard, 128), BF16),
        pltpu.VMEM((g.deep, jobs, 2, shard, 128), BF16),
        pltpu.VMEM((g.reps, jobs, 2, shard, 128) if g.reps > 1 else (1, 16, 128), BF16),
        pltpu.VMEM((jobs, 2, R, 128), BF16),
        dma((half,)), dma((half,)), dma((5,)), dma((4,)), dma((4,)),
        dma((2,)), dma((2,)), dma((2, 2, half)), dma((2, half)), dma((2, half)), dma((2,)), dma((2,)), dma((jobs, 9)), dma((jobs, 9)), dma((jobs, 2)),
        pltpu.SemaphoreType.REGULAR((g.parts,)),
    ]
    anywhere = pl.BlockSpec(memory_space=pl.ANY)
    vmem = pl.BlockSpec(memory_space=pltpu.VMEM)
    field = jax.ShapeDtypeStruct((1,) + boards.shape, BF16)
    fields = jax.ShapeDtypeStruct((2,) + boards.shape, BF16)
    grad = jax.ShapeDtypeStruct((2, 9 * C, 128), BF16)
    pair = jax.ShapeDtypeStruct(gains.shape, F32)
    hidden, igrads, k1, k2, gg, bg = pl.pallas_call(
        functools.partial(kernel, g),
        out_shape=(fields, fields, grad, grad, pair, pair),
        in_specs=[anywhere] * 7,
        out_specs=(anywhere, anywhere, anywhere, anywhere, vmem, vmem),
        scratch_shapes=scratch,
        compiler_params=pltpu.CompilerParams(collective_id=0, has_side_effects=True, vmem_limit_bytes=(63 * 16 + 14) * 2**16),
    )(
        boards, cotangent, counts.T, kernel_one.reshape(tall_kernel), kernel_two.reshape(tall_kernel), gains, biases
    )

    grad = jax.ShapeDtypeStruct(flat_kernel, F32)
    hidden, igrads, k1, k2, gg, bg = pl.pallas_call(
        finish,
        out_shape=(field, field, grad, grad, pair, pair),
        in_specs=[anywhere] * 6,
        out_specs=(anywhere,) * 6,
        scratch_shapes=[
            pltpu.VMEM((2,) + boards.shape, BF16),
            pltpu.VMEM((2, 2, 9 * C, 128), BF16),
            pltpu.VMEM((2, 9, C, C), F32),
            pltpu.VMEM((2,) + gains.shape, F32),
            dma((2, micro)), dma((2, micro)), dma((2,)), dma((2, 9)), dma((2,)), dma((2,)),
        ],
        compiler_params=pltpu.CompilerParams(vmem_limit_bytes=(63 * 16 + 14) * 2**16),
    )(hidden, igrads, k1, k2, gg, bg)
    return hidden, igrads, k1.reshape(kernel_one.shape), k2.reshape(kernel_two.shape), gg, bg


def finish(hidden, igrads, k1, k2, gg, bg, hidden_out, igrads_out, k1_out, k2_out, gg_out, bg_out, fields, narrow, wide, small, *sems):
    sem_in, sem_out, sem_k, sem_kout, sem_s, sem_sout = sems
    C = wide.shape[2]
    copies = pltpu.make_async_copy
    loads, stores = [], []
    for q, (src, dst) in enumerate(((gg, gg_out), (bg, bg_out))):
        loads.append(copies(src, small.at[q], sem_s.at[q]))
        stores.append(copies(small.at[q], dst, sem_sout.at[q]))
    kernels = [copies(src, narrow.at[q], sem_k.at[q]) for q, src in enumerate((k1, k2))]
    for q, (src, dst) in enumerate(((hidden, hidden_out), (igrads, igrads_out))):
        for m in range(src.shape[1]):
            loads.append(copies(src.at[0, m], fields.at[q, m], sem_in.at[q, m]))
            stores.append(copies(fields.at[q, m], dst.at[0, m], sem_out.at[q, m]))
    for c in kernels + loads:
        c.start()
    wides = []
    for q, dst in enumerate((k1_out, k2_out)):
        kernels[q].wait()
        for t in range(9):
            for h in range(2):
                wide[q, t, :, pl.ds(128 * h, 128)] = narrow[q, h, pl.ds(t * C, C), :].astype(F32)
            c = copies(wide.at[q, t], dst.at[0, t], sem_kout.at[q, t])
            c.start()
            wides.append(c)
    for load, store in zip(loads, stores):
        load.wait()
        store.start()
    for c in stores + wides:
        c.wait()


def solution(mesh):
    return jax.shard_map(
        functools.partial(local, mesh.shape["dp"]),
        mesh=mesh,
        in_specs=(
            P(None, "dp", None, None, None),
            P(None, "dp", None, None, None),
            P(None, "dp"),
            P("section", None, None, None, None),
            P("section", None, None, None, None),
            P("section", None, None),
            P("section", None, None),
        ),
        out_specs=(
            P("section", None, "dp", None, None, None),
            P("section", None, "dp", None, None, None),
            P("section", None, None, None, None),
            P("section", None, None, None, None),
            P("section", None, None),
            P("section", None, None),
        ),
        check_vma=False,
    )
```
